128 devices in a mesh: frame: 8 (over y, core), region: 16 (over z, x).
Axes of the slice: x: 4, y: 4, z: 4, core: 2. Of those that a mesh axis runs over, the one named last changes fastest.
Arguments:
- queries: bfloat16 [8, 4096, 3072], P('frame', 'region'), may hold values from -54 to 54
- keys: bfloat16 [8, 4096, 3072], P('frame', 'region'), may hold values from -18 to 18
- values: bfloat16 [8, 4096, 3072], P('frame', 'region'), may hold values from -6 to 6
- head_kind: int32 [24], replicated, may hold values from 0 to 1, as said below
- spatial_mask: int32 [24, 32, 32], replicated, may hold values 0 or 1
- temporal_mask: int32 [24, 8, 8], replicated, may hold values 0 or 1
- frame_valid: int32 [8], replicated, may hold values from 0 to 1, as said below
Outputs:
- attended: bfloat16 [8, 4096, 3072], P('frame', 'region')
The draws below stay inside these ranges and needn't reach their ends.
Inputs may be any that keep to these rules, and one draw needn't show every extreme that they name: `head_kind`: exactly 12 entries are 1. `frame_valid`: the last frame is always padding.
All inputs are finite; a program needn't handle non-finite values.
Results may differ from the reference program's by a relative error of at most 0.01.
Values may be sent and summed in bfloat16 or wider, within the bound.
No kernel may reach another device: no remote copies, remote signals or barrier semaphores. Data moves between devices by JAX's collectives and lax.ppermute only.
A program may use at most 192 MiB of HBM per device.

```python
import jax
import jax.numpy as jnp
from jax import lax

HEADS = 24
HEAD_DIM = 128
TEMP_HEADS = 12
BLK = 128
D = 3072
FRAMES = 8
FRAME_TOK = 4096
NBLK = 32


def shared_normal(key):
    shape = (FRAMES, FRAME_TOK, HEADS * HEAD_DIM)
    base = jax.random.truncated_normal(key, -6.0, 6.0, shape, jnp.float32)
    return base


def draw_keys(key, part):
    base = shared_normal(key)
    result = base
    return result.astype(jnp.bfloat16)


def draw_queries(key, part):
    base = shared_normal(key)
    key = jax.random.fold_in(key, 12)
    shape = base.shape
    result = jax.random.truncated_normal(key, -6.0, 6.0, shape, jnp.float32)
    return result.astype(jnp.bfloat16)


def draw_head_kind(key, part):
    key = jax.random.fold_in(key, 13)
    order = jax.random.permutation(key, HEADS)
    return (order < TEMP_HEADS).astype(jnp.int32)


def draw_frame_valid(key, part):
    key = jax.random.fold_in(key, 14)
    marks = jax.random.randint(key, (FRAMES,), 0, 4)
    last = jnp.arange(FRAMES) == FRAMES - 1
    return jnp.where(last, 0, (marks > 0).astype(jnp.int32)).astype(jnp.int32)


def with_ends(entries, own_key, smallest, largest):
    longest = entries.shape.index(max(entries.shape))
    spots = []
    for shift in (0, 1):
        where = [jax.random.randint(jax.random.fold_in(own_key, axis), (), 0, length) for axis, length in enumerate(entries.shape)]
        where[longest] = (where[longest] + shift) % entries.shape[longest]
        spots.append(tuple(where))
    return entries.at[spots[0]].set(smallest).at[spots[1]].set(largest)


def steps_of(own_key, dims, cuts, least, largest):
    level = 1.0
    for dim, blocks in cuts:
        steps = jax.random.uniform(jax.random.fold_in(jax.random.fold_in(own_key, 6), dim), (blocks,), jnp.float32, least / len(cuts), largest / len(cuts))
        level = level * jnp.repeat(jnp.exp(steps), dims[dim] // blocks).reshape((-1,) + (1,) * (len(dims) - 1 - dim))
    return level


def centred(rng, dims, scale, bound, cuts=(), held_as=jnp.bfloat16):
    values = scale * jax.random.normal(rng, dims, jnp.float32)
    if cuts:
        values = values * steps_of(rng, dims, cuts, -0.22, 0.18)
    return jnp.clip(values, -bound, bound).astype(held_as)


def setup_inputs(seed: int = 0) -> dict:
    seeds = jax.random.split(jax.random.key(seed), 8)
    queries = draw_queries(jax.random.fold_in(seeds[7], 71), 0)
    keys = draw_keys(jax.random.fold_in(seeds[7], 71), 0)
    values = centred(seeds[2], (FRAMES, FRAME_TOK, D), 1.0, 6.0, ((0, 8), (1, 16)))
    head_kind = draw_head_kind(jax.random.fold_in(seeds[7], 71), 0)
    spatial_mask = with_ends((jax.random.randint(seeds[4], (HEADS, NBLK, NBLK), 0, 2) < 1).astype(jnp.int32), jax.random.fold_in(seeds[4], 1), 0, 1)
    temporal_mask = with_ends((jax.random.randint(seeds[5], (HEADS, FRAMES, FRAMES), 0, 2) < 1).astype(jnp.int32), jax.random.fold_in(seeds[5], 1), 0, 1)
    frame_valid = draw_frame_valid(jax.random.fold_in(seeds[7], 71), 0)
    return {"queries": queries, "keys": keys, "values": values, "head_kind": head_kind, "spatial_mask": spatial_mask, "temporal_mask": temporal_mask, "frame_valid": frame_valid}


def softmax_weights(scores, allowed):
    masked = jnp.where(allowed, scores, -jnp.inf)
    top = jnp.max(masked, axis=-1, keepdims=True)
    expo = jnp.where(allowed, jnp.exp(masked - top), 0.0)
    return (expo / jnp.sum(expo, axis=-1, keepdims=True)).astype(jnp.bfloat16)


def reference(queries, keys, values, head_kind, spatial_mask, temporal_mask, frame_valid):
    scale = 1.0 / (HEAD_DIM ** 0.5)
    shape4 = (FRAMES, FRAME_TOK, HEADS, HEAD_DIM)
    q_heads = queries.reshape(shape4)
    k_heads = keys.reshape(shape4)
    v_heads = values.reshape(shape4)
    block_ids = jnp.arange(NBLK)
    eye_frames = jnp.arange(FRAMES)[:, None] == jnp.arange(FRAMES)[None, :]

    def one_head(head):
        q_one = lax.dynamic_index_in_dim(q_heads, head, 2, False)
        k_one = lax.dynamic_index_in_dim(k_heads, head, 2, False)
        v_one = lax.dynamic_index_in_dim(v_heads, head, 2, False)

        def spatial(unused):
            blocks = lax.dynamic_index_in_dim(spatial_mask, head, 0, False)
            allowed_blocks = (blocks == 1) | (block_ids[:, None] == block_ids[None, :])
            allowed = jnp.repeat(jnp.repeat(allowed_blocks, BLK, 0), BLK, 1)

            def one_frame(frame):
                q_f = lax.dynamic_index_in_dim(q_one, frame, 0, False)
                k_f = lax.dynamic_index_in_dim(k_one, frame, 0, False)
                v_f = lax.dynamic_index_in_dim(v_one, frame, 0, False)
                scores = jnp.dot(q_f, k_f.T, preferred_element_type=jnp.float32) * scale
                weights = softmax_weights(scores, allowed)
                return jnp.dot(weights, v_f, preferred_element_type=jnp.float32).astype(jnp.bfloat16)

            return lax.map(one_frame, jnp.arange(FRAMES))

        def temporal(unused):
            pairs = lax.dynamic_index_in_dim(temporal_mask, head, 0, False)
            allowed = ((pairs == 1) & (frame_valid[None, :] == 1)) | eye_frames
            scores = jnp.einsum("fnd,gnd->nfg", q_one.astype(jnp.float32), k_one.astype(jnp.float32)) * scale
            weights = softmax_weights(scores, allowed[None])
            result = jnp.einsum("nfg,gnd->fnd", weights.astype(jnp.float32), v_one.astype(jnp.float32))
            return result.astype(jnp.bfloat16)

        kind = lax.dynamic_index_in_dim(head_kind, head, 0, False)
        return lax.cond(kind == 0, spatial, temporal, 0)

    outputs = lax.map(one_head, jnp.arange(HEADS))
    return jnp.transpose(outputs, (1, 2, 0, 3)).reshape(FRAMES, FRAME_TOK, HEADS * HEAD_DIM)
```

```python
import functools

import jax
import jax.numpy as jnp
from jax import lax
from jax.experimental import pallas as pl
from jax.experimental.pallas import tpu as pltpu
from jax.sharding import PartitionSpec as P

HEADS = 24
TEMP_HEADS = 12
SPAT_HEADS = HEADS - TEMP_HEADS
BLK = 128
HEAD = 128
RING = 4
GROUP = SPAT_HEADS // RING
FRAMES = 8
ROWS = 256
PART = ROWS // FRAMES
WIDTH = HEADS * HEAD
NEG = -1e30
LOG2_SCALE = 1.4426950408889634 / HEAD**0.5
AXES = ("frame", "region")
VMEM = 56 * 1024 * 1024
BF16 = jnp.bfloat16
F32 = jnp.float32
ANY = pl.BlockSpec(memory_space=pl.ANY)
SMEM = pl.BlockSpec(memory_space=pltpu.SMEM)


def flat(y, core, z, x):
    return ((y * 2 + core) * RING + z) * RING + x


def axis_groups(first):
    groups = []
    for y in range(RING):
        for core in range(2):
            along_x = (core == 0) == first
            for other in range(RING):
                groups.append([
                    flat(y, core, other, i) if along_x else flat(y, core, i, other)
                    for i in range(RING)
                ])
    return groups


def ring_pairs(first, shift):
    pairs = []
    for group in axis_groups(first):
        for i in range(RING):
            pairs.append((group[i], group[(i + shift) % RING]))
    return sorted(pairs)


def swap(tensor):
    return lax.all_to_all(tensor, AXES, 0, 0, tiled=True, axis_index_groups=axis_groups(True))


def shift(tensor, step):
    return lax.ppermute(tensor, AXES, ring_pairs(False, step))


def columns(index):
    return pl.ds(pl.multiple_of(index * HEAD, HEAD), HEAD)


def pack_kv(kind, k_ref, v_ref, kv_ref, order_ref, sem):
    spatial = jnp.int32(0)
    temporal = jnp.int32(0)
    for head in range(HEADS):
        one = kind[head]
        order_ref[jnp.where(one == 1, SPAT_HEADS + temporal, spatial)] = head

        @pl.when(one == 0)
        def _(spatial=spatial, head=head):
            group, place = spatial // GROUP, spatial % GROUP
            for which, ref in enumerate((k_ref, v_ref)):
                pltpu.make_async_copy(
                    ref.at[:, pl.ds(head * HEAD, HEAD)], kv_ref.at[group, which, place], sem
                ).start()

        spatial += 1 - one
        temporal += one
    pltpu.make_async_copy(kv_ref, kv_ref, sem).wait()


def pack_rest(kind, q_ref, k_ref, v_ref, sq_ref, tm_ref, sem_s, sem_t):
    spatial = jnp.int32(0)
    temporal = jnp.int32(0)
    for head in range(HEADS):
        one = kind[head]

        @pl.when(one == 0)
        def _(spatial=spatial, head=head):
            pltpu.make_async_copy(
                q_ref.at[:, pl.ds(head * HEAD, HEAD)],
                sq_ref.at[spatial // GROUP, spatial % GROUP],
                sem_s,
            ).start()

        @pl.when(one == 1)
        def _(temporal=temporal, head=head):
            for which, ref in enumerate((q_ref, k_ref, v_ref)):
                pltpu.make_async_copy(
                    ref.at[:, pl.ds(head * HEAD, HEAD)],
                    tm_ref.at[:, columns(which * TEMP_HEADS + temporal)],
                    sem_t,
                ).start()

        spatial += 1 - one
        temporal += one
    pltpu.make_async_copy(sq_ref, sq_ref, sem_s).wait()
    pltpu.make_async_copy(tm_ref, tm_ref, sem_t).wait()


def place_temporal(kind, src_ref, out_ref, sem):
    temporal = jnp.int32(0)
    for head in range(HEADS):
        one = kind[head]

        @pl.when(one == 1)
        def _(temporal=temporal, head=head):
            pltpu.make_async_copy(
                src_ref.at[:, columns(temporal)], out_ref.at[:, pl.ds(head * HEAD, HEAD)], sem
            ).start()

        temporal += one
    pltpu.make_async_copy(src_ref, src_ref, sem).wait()


def place_spatial(kind, src_ref, base_ref, out_ref, sem):
    spatial = jnp.int32(0)
    for head in range(HEADS):
        one = kind[head]

        @pl.when(one == 0)
        def _(spatial=spatial, head=head):
            pltpu.make_async_copy(
                src_ref.at[spatial // GROUP, spatial % GROUP],
                out_ref.at[:, pl.ds(head * HEAD, HEAD)],
                sem,
            ).start()

        spatial += 1 - one
    pltpu.make_async_copy(src_ref, src_ref, sem).wait()


def region_of(where, piece, ring):
    return jnp.where(where[0] == 0, ring * RING + piece, piece * RING + ring)


def attend(chunks, has_state, last, order, where, q_ref, bias_ref, *refs):
    kv_refs = refs[: len(chunks)]
    refs = refs[len(chunks):]
    if has_state:
        acc_in, stat_in = refs[:2]
        refs = refs[2:]
    if last:
        (out_ref,) = refs[:1]
        refs = refs[1:]
    else:
        acc_out, stat_out = refs[:2]
        refs = refs[2:]
    keys, vals = refs
    ring = where[1]
    row = 0
    for (offset, pieces), kv_ref in zip(chunks, kv_refs):
        source = (ring + offset) % RING
        for slot, piece in enumerate(pieces):
            region = region_of(where, piece, source)
            keys[pl.ds(row, ROWS), :HEAD] = kv_ref[slot, 0, 0]
            vals[pl.ds(row, ROWS), :HEAD] = kv_ref[slot, 1, 0]
            for half in range(ROWS // BLK):
                line = bias_ref[0, pl.ds(region * (ROWS // BLK) + half, 1), :]
                keys[pl.ds(row + half * BLK, BLK), HEAD:] = jnp.broadcast_to(
                    line, (BLK, HEAD)
                ).astype(BF16)
            row += ROWS
    vals[:, HEAD:] = jnp.ones((row, HEAD), BF16)
    lane = lax.broadcasted_iota(jnp.int32, (ROWS, HEAD), 1)
    half = lax.broadcasted_iota(jnp.int32, (ROWS, HEAD), 0) // BLK
    for piece in range(RING):
        block = region_of(where, piece, ring) * (ROWS // BLK) + half
        mark = jnp.where(lane == block, 1.0, 0.0).astype(BF16)
        query = jnp.concatenate([q_ref[piece, 0], mark], axis=1)
        scores = lax.dot_general(
            query, keys[...], (((1,), (1,)), ((), ())), preferred_element_type=F32
        )
        top = jnp.max(scores, axis=1, keepdims=True)
        if has_state:
            stat = stat_in[0, piece]
            old = stat[:, :1]
            top = jnp.maximum(top, old)
        weights = jnp.exp2((scores - top) * LOG2_SCALE).astype(BF16)
        both = jnp.dot(weights, vals[...], preferred_element_type=F32)
        total, sums = both[:, :HEAD], both[:, HEAD:]
        if has_state:
            decay = jnp.exp2((old - top) * LOG2_SCALE)
            total = total + acc_in[0, piece] * decay
            sums = sums + stat[:, HEAD - 1:] * decay
        if last:
            out_ref[piece, 0] = (total / sums).astype(BF16)
        else:
            acc_out[0, piece] = total
            stat_out[0, piece] = jnp.where(lane < HEAD // 2, top, sums)


def attention(order, where, bias, queries, chunks, arrays, state=None, last=False):
    keys = sum(len(pieces) for _, pieces in chunks) * ROWS
    kv_specs = [
        pl.BlockSpec((len(pieces), 2, 1, ROWS, HEAD), lambda h, o, w: (0, 0, h, 0, 0))
        for _, pieces in chunks
    ]
    q_spec = pl.BlockSpec((RING, 1, ROWS, HEAD), lambda h, o, w: (0, h, 0, 0))
    state_spec = pl.BlockSpec((1, RING, ROWS, HEAD), lambda h, o, w: (h, 0, 0, 0))
    bias_spec = pl.BlockSpec(
        (1, bias.shape[1], HEAD), lambda h, o, w: (o[w[2] * GROUP + h], 0, 0)
    )
    state_shape = jax.ShapeDtypeStruct((GROUP, RING, ROWS, HEAD), F32)
    flops = 8 * GROUP * RING * ROWS * keys * HEAD
    return pl.pallas_call(
        functools.partial(attend, chunks, state is not None, last),
        grid_spec=pltpu.PrefetchScalarGridSpec(
            num_scalar_prefetch=2,
            grid=(GROUP,),
            in_specs=[q_spec, bias_spec] + kv_specs + [state_spec] * (0 if state is None else 2),
            out_specs=q_spec if last else [state_spec] * 2,
            scratch_shapes=[pltpu.VMEM((keys, 2 * HEAD), BF16)] * 2,
        ),
        out_shape=jax.ShapeDtypeStruct(queries.shape, BF16) if last else [state_shape] * 2,
        compiler_params=pltpu.CompilerParams(vmem_limit_bytes=VMEM),
        cost_estimate=pl.CostEstimate(flops=flops, bytes_accessed=4 << 20, transcendentals=0),
        name="spatial_attention",
    )(order, where, queries, bias, *arrays, *(state or ()))


def attend_time(order, bias_ref, q_ref, k_ref, v_ref, out_ref):
    lane = lax.broadcasted_iota(jnp.int32, (ROWS, HEAD), 1)
    row = lax.broadcasted_iota(jnp.int32, (ROWS, HEAD), 0)
    frame, place = row // PART, row % PART
    mark = jnp.where((lane == frame) | (lane == FRAMES + place), 1.0, 0.0).astype(BF16)
    apart = jnp.where(
        (lane >= FRAMES) & (lane < FRAMES + PART) & (lane != FRAMES + place), NEG, 0.0
    )
    pairs = jnp.broadcast_to(bias_ref[0][:, None, :], (FRAMES, PART, HEAD)).reshape(ROWS, HEAD)
    query = jnp.concatenate([q_ref[...], mark], axis=1)
    keys = jnp.concatenate([k_ref[...], (pairs + apart).astype(BF16)], axis=1)
    vals = jnp.concatenate([v_ref[...], jnp.ones((ROWS, HEAD), BF16)], axis=1)
    scores = lax.dot_general(query, keys, (((1,), (1,)), ((), ())), preferred_element_type=F32)
    top = jnp.max(scores, axis=1, keepdims=True)
    weights = jnp.exp2((scores - top) * LOG2_SCALE).astype(BF16)
    both = jnp.dot(weights, vals, preferred_element_type=F32)
    out_ref[...] = (both[:, :HEAD] / both[:, HEAD:]).astype(BF16)


def time_attention(order, bias, gathered):
    def at(which):
        return pl.BlockSpec((ROWS, HEAD), lambda h, o: (0, which * TEMP_HEADS + h))

    return pl.pallas_call(
        attend_time,
        grid_spec=pltpu.PrefetchScalarGridSpec(
            num_scalar_prefetch=1,
            grid=(TEMP_HEADS,),
            in_specs=[pl.BlockSpec((1, FRAMES, HEAD), lambda h, o: (o[SPAT_HEADS + h], 0, 0))]
            + [at(which) for which in range(3)],
            out_specs=at(0),
        ),
        out_shape=jax.ShapeDtypeStruct((ROWS, TEMP_HEADS * HEAD), BF16),
        compiler_params=pltpu.CompilerParams(vmem_limit_bytes=VMEM),
        cost_estimate=pl.CostEstimate(flops=4 << 30, bytes_accessed=4 << 20, transcendentals=0),
        name="temporal_attention",
    )(order, bias, gathered, gathered, gathered)


def moved(count):
    return pl.CostEstimate(flops=0, bytes_accessed=count, transcendentals=0)


def shards(queries, keys, values, head_kind, spatial_mask, temporal_mask, frame_valid):
    rows, width = queries.shape[1:]
    queries, keys, values = (t.reshape(rows, width) for t in (queries, keys, values))
    dma = pltpu.SemaphoreType.DMA
    core = lax.axis_index("frame") % 2
    region = lax.axis_index("region")
    place_z, place_x = region // RING, region % RING
    own = jnp.where(core == 0, place_x, place_z)
    ring = jnp.where(core == 0, place_z, place_x)
    where = jnp.stack([core, ring, own]).astype(jnp.int32)

    kv, order = pl.pallas_call(
        pack_kv,
        in_specs=[SMEM, ANY, ANY],
        out_specs=[ANY, SMEM],
        out_shape=[
            jax.ShapeDtypeStruct((RING, 2, GROUP, ROWS, HEAD), BF16),
            jax.ShapeDtypeStruct((HEADS,), jnp.int32),
        ],
        scratch_shapes=[dma],
        cost_estimate=moved(3 << 20),
        name="pack_keys_values",
    )(head_kind, keys, values)
    kv = swap(kv)
    sq, tm = pl.pallas_call(
        pack_rest,
        in_specs=[SMEM, ANY, ANY, ANY],
        out_specs=[ANY, ANY],
        out_shape=[
            jax.ShapeDtypeStruct((RING, GROUP, ROWS, HEAD), BF16),
            jax.ShapeDtypeStruct((ROWS, 3 * TEMP_HEADS * HEAD), BF16),
        ],
        scratch_shapes=[dma, dma],
        cost_estimate=moved(6 << 20),
        name="pack_rest",
    )(head_kind, queries, keys, values)
    sq = swap(sq)
    tm = lax.all_to_all(tm, "frame", 0, 0, tiled=True)

    blocks = spatial_mask.shape[1]
    same = jnp.eye(blocks, dtype=jnp.bool_)[None]
    bias = jnp.where((jnp.swapaxes(spatial_mask, 1, 2) == 1) | same, 0.0, NEG).astype(F32)
    bias = jnp.pad(bias, ((0, 0), (0, 0), (0, HEAD - blocks)))
    alike = jnp.eye(FRAMES, dtype=jnp.bool_)[None]
    seen = (jnp.swapaxes(temporal_mask, 1, 2) == 1) & (frame_valid[None, :, None] == 1)
    time_bias = jnp.where(seen | alike, 0.0, NEG).astype(F32)
    time_bias = jnp.pad(time_bias, ((0, 0), (0, 0), (0, HEAD - FRAMES)))

    whole = tuple(range(RING))
    half = RING // 2
    right, left = shift(kv, 1), shift(kv, RING - 1)
    state = attention(order, where, bias, sq, [(0, whole)], [kv])
    right2, left2 = shift(right[:half], 1), shift(left[half:], RING - 1)
    state = attention(
        order, where, bias, sq, [(RING - 1, whole), (1, whole)], [right, left], state
    )
    spatial = attention(
        order, where, bias, sq, [(2, whole[:half]), (2, whole[half:])], [right2, left2], state, True
    )
    time_out = time_attention(order, time_bias, tm)
    time_out = lax.all_to_all(time_out, "frame", 0, 0, tiled=True)
    out_shape = jax.ShapeDtypeStruct((rows, width), BF16)
    base = pl.pallas_call(
        place_temporal,
        in_specs=[SMEM, ANY],
        out_specs=ANY,
        out_shape=out_shape,
        scratch_shapes=[dma],
        cost_estimate=moved(2 << 20),
        name="place_temporal",
    )(head_kind, time_out)
    spatial = swap(spatial)
    result = pl.pallas_call(
        place_spatial,
        in_specs=[SMEM, ANY, ANY],
        out_specs=ANY,
        out_shape=out_shape,
        scratch_shapes=[dma],
        input_output_aliases={2: 0},
        cost_estimate=moved(2 << 20),
        name="place_spatial",
    )(head_kind, spatial, base)
    return result[None]


def solution(mesh):
    wide = P("frame", "region", None)
    return jax.shard_map(
        shards,
        mesh=mesh,
        in_specs=(wide, wide, wide, P(), P(), P(), P()),
        out_specs=wide,
        check_vma=False,
    )
```

```python
import functools

import jax
import jax.numpy as jnp
from jax import lax
from jax.experimental import pallas as pl
from jax.experimental.pallas import tpu as pltpu
from jax.sharding import PartitionSpec as P

HEADS = 24
TEMP_HEADS = 12
SPAT_HEADS = HEADS - TEMP_HEADS
BLK = 128
HEAD = 128
RING = 4
GROUP = SPAT_HEADS // RING
FRAMES = 8
ROWS = 256
PART = ROWS // FRAMES
WIDTH = HEADS * HEAD
NEG = -1e30
LEVEL = 32
LARGE = 2.0**100
STEP = 1024
TIME_STEP = 6
LOG2_SCALE = 1.4426950408889634 / HEAD**0.5
AXES = ("frame", "region")
VMEM = 56 * 1024 * 1024
BF16 = jnp.bfloat16
F32 = jnp.float32
ANY = pl.BlockSpec(memory_space=pl.ANY)
SMEM = pl.BlockSpec(memory_space=pltpu.SMEM)


def flat(y, core, z, x):
    return ((y * 2 + core) * RING + z) * RING + x


def axis_groups(first):
    groups = []
    for y in range(RING):
        for core in range(2):
            along_x = (core == 0) == first
            for other in range(RING):
                groups.append([
                    flat(y, core, other, i) if along_x else flat(y, core, i, other)
                    for i in range(RING)
                ])
    return groups


def ring_pairs(first, shift):
    pairs = []
    for group in axis_groups(first):
        for i in range(RING):
            pairs.append((group[i], group[(i + shift) % RING]))
    return sorted(pairs)


def swap(tensor):
    return lax.all_to_all(tensor, AXES, 0, 0, tiled=True, axis_index_groups=axis_groups(True))


def shift(tensor, step):
    return lax.ppermute(tensor, AXES, ring_pairs(False, step))


def columns(index):
    return pl.ds(pl.multiple_of(index * HEAD, HEAD), HEAD)


def pack_kv(kind, k_ref, v_ref, kv_ref, order_ref, held, sem_in, sem_out):
    spatial = jnp.int32(0)
    temporal = jnp.int32(0)
    for head in range(HEADS):
        one = kind[head]

        @pl.when(one == 0)
        def _(spatial=spatial, head=head):
            group, place = spatial // GROUP, spatial % GROUP
            for which, ref in enumerate((k_ref, v_ref)):
                pltpu.make_async_copy(
                    ref.at[:, pl.ds(head * HEAD, HEAD)],
                    held.at[which, group, place],
                    sem_in.at[which],
                ).start()

        order_ref[jnp.where(one == 1, SPAT_HEADS + temporal, spatial)] = head
        spatial += 1 - one
        temporal += one
    copies = [
        pltpu.make_async_copy(held.at[which], kv_ref.at[:, which], sem_out.at[which])
        for which in range(2)
    ]
    for which, copy in enumerate(copies):
        pltpu.make_async_copy(held.at[which], held.at[which], sem_in.at[which]).wait()
        copy.start()
    for copy in copies:
        copy.wait()


def pack_rest(kind, order, q_ref, k_ref, v_ref, sq_ref, tm_ref, held_s, held_t, sem_in, sem_out):
    spatial = jnp.int32(0)
    temporal = jnp.int32(0)
    for head in range(HEADS):
        one = kind[head]

        @pl.when(one == 0)
        def _(spatial=spatial, head=head):
            pltpu.make_async_copy(
                q_ref.at[:, pl.ds(head * HEAD, HEAD)],
                held_s.at[spatial // GROUP, spatial % GROUP],
                sem_in.at[0],
            ).start()

        @pl.when(one == 1)
        def _(temporal=temporal, head=head):
            for which, ref in enumerate((q_ref, k_ref, v_ref)):
                pltpu.make_async_copy(
                    ref.at[:, pl.ds(head * HEAD, HEAD)],
                    held_t.at[:, columns(which * TEMP_HEADS + temporal)],
                    sem_in.at[1],
                ).start()

        spatial += 1 - one
        temporal += one
    copies = []
    for which, (held, ref) in enumerate(((held_s, sq_ref), (held_t, tm_ref))):
        pltpu.make_async_copy(held, held, sem_in.at[which]).wait()
        copies.append(pltpu.make_async_copy(held, ref, sem_out.at[which]))
        copies[-1].start()
    for copy in copies:
        copy.wait()


def place_temporal(kind, src_ref, out_ref, held, sem_in, sem_out):
    copy = pltpu.make_async_copy(src_ref, held, sem_in)
    copy.start()
    copy.wait()
    temporal = jnp.int32(0)
    for head in range(HEADS):
        one = kind[head]

        @pl.when(one == 1)
        def _(temporal=temporal, head=head):
            pltpu.make_async_copy(
                held.at[:, columns(temporal)], out_ref.at[:, pl.ds(head * HEAD, HEAD)], sem_out
            ).start()

        temporal += one
    pltpu.make_async_copy(held, held, sem_out).wait()


def place_spatial(kind, src_ref, base_ref, out_ref, held, sem_in, sem_out):
    copy = pltpu.make_async_copy(src_ref, held, sem_in)
    copy.start()
    copy.wait()
    spatial = jnp.int32(0)
    for head in range(HEADS):
        one = kind[head]

        @pl.when(one == 0)
        def _(spatial=spatial, head=head):
            pltpu.make_async_copy(
                held.at[spatial // GROUP, spatial % GROUP],
                out_ref.at[:, pl.ds(head * HEAD, HEAD)],
                sem_out,
            ).start()

        spatial += 1 - one
    pltpu.make_async_copy(held, held, sem_out).wait()


def region_of(where, piece, ring):
    return jnp.where(where[0] == 0, ring * RING + piece, piece * RING + ring)


def mark_queries(where, q_ref, k_ref, marked_ref):
    lane = lax.broadcasted_iota(jnp.int32, (ROWS, HEAD), 1)
    half = lax.broadcasted_iota(jnp.int32, (ROWS, HEAD), 0) // BLK
    for piece in range(RING):
        block = region_of(where, piece, where[1]) * (ROWS // BLK) + half
        query = q_ref[piece, 0]
        level = jnp.sum(
            query.astype(F32) * k_ref[piece, 0, 0].astype(F32), axis=1, keepdims=True
        )
        mark = jnp.where(lane == block, 1.0, jnp.where(lane == LEVEL, -level, 0.0))
        rows = pl.ds(piece * ROWS, ROWS)
        marked_ref[0, rows, :HEAD] = query
        marked_ref[0, rows, HEAD:] = mark.astype(BF16)


def mark_keys(where, bias_ref, region, keys, row):
    for half in range(ROWS // BLK):
        line = bias_ref[0, pl.ds(region * (ROWS // BLK) + half, 1), :]
        keys[pl.ds(row + half * BLK, BLK), HEAD:] = jnp.broadcast_to(line, (BLK, HEAD)).astype(BF16)


def attend_again(all_chunks, where, bias_ref, marked_ref, kv_all, out_ref, keys, vals, top_ref, sum_ref, acc_ref, sem):
    head = pl.program_id(0)
    lane = lax.broadcasted_iota(jnp.int32, (ROWS, 2 * HEAD), 1)
    top_ref[...] = jnp.full(top_ref.shape, -3e38, F32)
    sum_ref[...] = jnp.zeros(sum_ref.shape, F32)
    acc_ref[...] = jnp.zeros(acc_ref.shape, F32)
    for (offset, pieces), kv_ref in zip(all_chunks, kv_all):
        source = (where[1] + offset) % RING

        @pl.loop(0, len(pieces))
        def _(slot, kv_ref=kv_ref, pieces=pieces, source=source):
            copies = [
                pltpu.make_async_copy(kv_ref.at[slot, 0, head], keys.at[:, :HEAD], sem.at[0]),
                pltpu.make_async_copy(kv_ref.at[slot, 1, head], vals, sem.at[1]),
            ]
            for copy in copies:
                copy.start()
            mark_keys(where, bias_ref, region_of(where, slot + pieces[0], source), keys, 0)
            for copy in copies:
                copy.wait()
            for piece in range(RING):
                rows = pl.ds(piece * ROWS, ROWS)
                query = marked_ref[0, rows, :]
                query = jnp.where(lane == HEAD + LEVEL, jnp.zeros_like(query), query)
                scores = lax.dot_general(
                    query, keys[...], (((1,), (1,)), ((), ())), preferred_element_type=F32
                )
                old = top_ref[rows, :]
                top = jnp.maximum(old, jnp.max(scores, axis=1, keepdims=True))
                decay = jnp.exp2((old - top) * LOG2_SCALE)
                weights = jnp.exp2((scores - top[:, :1]) * LOG2_SCALE).astype(BF16)
                sums = jnp.sum(weights.astype(F32), axis=1, keepdims=True)
                total = jnp.dot(weights, vals[...], preferred_element_type=F32)
                top_ref[rows, :] = top
                sum_ref[rows, :] = sum_ref[rows, :] * decay + sums
                acc_ref[rows, :] = acc_ref[rows, :] * decay + total

    for piece in range(RING):
        rows = pl.ds(piece * ROWS, ROWS)
        out_ref[piece, 0] = (acc_ref[rows, :] / sum_ref[rows, :]).astype(BF16)


def attend(chunks, all_chunks, first, order, where, bias_ref, *refs):
    kv_refs, refs = refs[: len(chunks)], refs[len(chunks):]
    last = all_chunks is not None
    if first:
        q_ref, marked_ref, state_ref, keys, vals = refs
        mark_queries(where, q_ref, kv_refs[0], marked_ref)
        state = jnp.zeros((HEAD + 8, RING * ROWS), F32)
    else:
        marked_ref, before_ref = refs[:2]
        state = before_ref[0]
        if last:
            kv_all, refs = refs[2:2 + len(all_chunks)], refs[2 + len(all_chunks):]
            out_ref, keys, vals = refs[:3]
        else:
            state_ref, keys, vals = refs[2:]
    row = 0
    for (offset, pieces), kv_ref in zip(chunks, kv_refs):
        source = (where[1] + offset) % RING
        for slot, piece in enumerate(pieces):
            keys[pl.ds(row, ROWS), :HEAD] = kv_ref[slot, 0, 0]
            mark_keys(where, bias_ref, region_of(where, piece, source), keys, row)
            vals[:HEAD, pl.ds(row, ROWS)] = kv_ref[slot, 1, 0].T
            row += ROWS
    vals[HEAD:, :] = jnp.ones((8, row), BF16)
    span = min(row, STEP)
    for start in range(0, row, span):
        scores = lax.dot_general(
            keys[pl.ds(start, span), :],
            marked_ref[0],
            (((1,), (1,)), ((), ())),
            preferred_element_type=F32,
        )
        weights = jnp.exp2(scores * LOG2_SCALE).astype(BF16)
        state += lax.dot_general(
            vals[:, pl.ds(start, span)],
            weights,
            (((1,), (0,)), ((), ())),
            preferred_element_type=F32,
        )
    if not last:
        state_ref[0] = state
        return
    sums = state[HEAD:HEAD + 1]
    result = state[:HEAD] / sums
    for piece in range(RING):
        out_ref[piece, 0] = result[:, piece * ROWS:(piece + 1) * ROWS].T.astype(BF16)
    fine = jnp.max(jnp.where(sums < LARGE, 0.0, 1.0)) == 0.0

    @pl.when(jnp.logical_not(fine))
    def _():
        attend_again(all_chunks, where, bias_ref, marked_ref, kv_all, out_ref, *refs[3:])


def attention(order, where, bias, chunks, arrays, queries=None, carried=None, everything=None):
    keys = sum(len(pieces) for _, pieces in chunks) * ROWS
    tokens = RING * ROWS
    kv_specs = [
        pl.BlockSpec((len(pieces), 2, 1, ROWS, HEAD), lambda h, o, w: (0, 0, h, 0, 0))
        for _, pieces in chunks
    ]
    bias_spec = pl.BlockSpec(
        (1, bias.shape[1], HEAD), lambda h, o, w: (o[w[2] * GROUP + h], 0, 0)
    )
    q_spec = pl.BlockSpec((RING, 1, ROWS, HEAD), lambda h, o, w: (0, h, 0, 0))
    marked_spec = pl.BlockSpec((1, tokens, 2 * HEAD), lambda h, o, w: (h, 0, 0))
    state_spec = pl.BlockSpec((1, HEAD + 8, tokens), lambda h, o, w: (h, 0, 0))
    marked_shape = jax.ShapeDtypeStruct((GROUP, tokens, 2 * HEAD), BF16)
    state_shape = jax.ShapeDtypeStruct((GROUP, HEAD + 8, tokens), F32)
    scratch = [pltpu.VMEM((keys, 2 * HEAD), BF16), pltpu.VMEM((HEAD + 8, keys), BF16)]
    all_chunks = None
    if queries is not None:
        more, more_specs = [queries], [q_spec]
        out_specs, out_shape = [marked_spec, state_spec], [marked_shape, state_shape]
    elif everything is None:
        more, more_specs = list(carried), [marked_spec, state_spec]
        out_specs, out_shape = state_spec, state_shape
    else:
        all_chunks, all_arrays = everything
        more = list(carried) + list(all_arrays)
        more_specs = [marked_spec, state_spec] + [ANY] * len(all_arrays)
        out_specs = q_spec
        out_shape = jax.ShapeDtypeStruct((RING, GROUP, ROWS, HEAD), BF16)
        scratch += [pltpu.VMEM((ROWS, 2 * HEAD), BF16), pltpu.VMEM((ROWS, HEAD), BF16)]
        scratch += [pltpu.VMEM((tokens, HEAD), F32)] * 3 + [pltpu.SemaphoreType.DMA((2,))]
    flops = 8 * GROUP * tokens * keys * HEAD
    return pl.pallas_call(
        functools.partial(attend, chunks, all_chunks, queries is not None),
        grid_spec=pltpu.PrefetchScalarGridSpec(
            num_scalar_prefetch=2,
            grid=(GROUP,),
            in_specs=[bias_spec] + kv_specs + more_specs,
            out_specs=out_specs,
            scratch_shapes=scratch,
        ),
        out_shape=out_shape,
        compiler_params=pltpu.CompilerParams(vmem_limit_bytes=VMEM),
        cost_estimate=pl.CostEstimate(flops=flops, bytes_accessed=4 << 20, transcendentals=0),
        name="spatial_attention",
    )(order, where, bias, *arrays, *more)


def attend_time(order, bias_ref, q_ref, k_ref, v_ref, out_ref):
    lane = lax.broadcasted_iota(jnp.int32, (ROWS, HEAD), 1)
    row = lax.broadcasted_iota(jnp.int32, (ROWS, HEAD), 0)
    frame, place = row // PART, row % PART
    mark = jnp.where((lane == frame) | (lane == FRAMES + place), 1.0, 0.0).astype(BF16)
    apart = jnp.where(
        (lane >= FRAMES) & (lane < FRAMES + PART) & (lane != FRAMES + place), NEG, 0.0
    )
    ones = jnp.ones((ROWS, HEAD), BF16)
    for slot in range(TIME_STEP):
        head = order[SPAT_HEADS + pl.program_id(0) * TIME_STEP + slot]
        at = slice(slot * HEAD, (slot + 1) * HEAD)
        pairs = jnp.broadcast_to(bias_ref[head][:, None, :], (FRAMES, PART, HEAD))
        pairs = pairs.reshape(ROWS, HEAD)
        query = jnp.concatenate([q_ref[:, at], mark], axis=1)
        keys = jnp.concatenate([k_ref[:, at], (pairs + apart).astype(BF16)], axis=1)
        vals = jnp.concatenate([v_ref[:, at], ones], axis=1)
        scores = lax.dot_general(
            query, keys, (((1,), (1,)), ((), ())), preferred_element_type=F32
        )
        top = jnp.max(scores, axis=1, keepdims=True)
        weights = jnp.exp2((scores - top) * LOG2_SCALE).astype(BF16)
        both = jnp.dot(weights, vals, preferred_element_type=F32)
        out_ref[:, at] = (both[:, :HEAD] / both[:, HEAD:]).astype(BF16)


def time_attention(order, bias, gathered):
    steps = TEMP_HEADS // TIME_STEP

    def at(which):
        return pl.BlockSpec((ROWS, TIME_STEP * HEAD), lambda h, o: (0, which * steps + h))

    return pl.pallas_call(
        attend_time,
        grid_spec=pltpu.PrefetchScalarGridSpec(
            num_scalar_prefetch=1,
            grid=(steps,),
            in_specs=[pl.BlockSpec(bias.shape, lambda h, o: (0, 0, 0))]
            + [at(which) for which in range(3)],
            out_specs=at(0),
        ),
        out_shape=jax.ShapeDtypeStruct((ROWS, TEMP_HEADS * HEAD), BF16),
        compiler_params=pltpu.CompilerParams(vmem_limit_bytes=VMEM),
        cost_estimate=pl.CostEstimate(flops=3 << 30, bytes_accessed=4 << 20, transcendentals=0),
        name="temporal_attention",
    )(order, bias, gathered, gathered, gathered)


def moved(count):
    return pl.CostEstimate(flops=0, bytes_accessed=count, transcendentals=0)


def shards(queries, keys, values, head_kind, spatial_mask, temporal_mask, frame_valid):
    rows, width = queries.shape[1:]
    queries, keys, values = (t.reshape(rows, width) for t in (queries, keys, values))
    dma = pltpu.SemaphoreType.DMA
    core = lax.axis_index("frame") % 2
    region = lax.axis_index("region")
    place_z, place_x = region // RING, region % RING
    own = jnp.where(core == 0, place_x, place_z)
    ring = jnp.where(core == 0, place_z, place_x)
    where = jnp.stack([core, ring, own]).astype(jnp.int32)

    pair = pltpu.SemaphoreType.DMA((2,))
    spatial_shape = (RING, GROUP, rows, HEAD)
    time_shape = (rows, TEMP_HEADS * HEAD)
    kv, order = pl.pallas_call(
        pack_kv,
        in_specs=[SMEM, ANY, ANY],
        out_specs=[ANY, SMEM],
        out_shape=[
            jax.ShapeDtypeStruct((RING, 2, GROUP, rows, HEAD), BF16),
            jax.ShapeDtypeStruct((HEADS,), jnp.int32),
        ],
        scratch_shapes=[pltpu.VMEM((2,) + spatial_shape, BF16), pair, pair],
        compiler_params=pltpu.CompilerParams(vmem_limit_bytes=VMEM),
        cost_estimate=moved(3 << 20),
        name="pack_keys_values",
    )(head_kind, keys, values)
    kv = swap(kv)
    sq, tm = pl.pallas_call(
        pack_rest,
        in_specs=[SMEM, SMEM, ANY, ANY, ANY],
        out_specs=[ANY, ANY],
        out_shape=[
            jax.ShapeDtypeStruct(spatial_shape, BF16),
            jax.ShapeDtypeStruct((rows, 3 * TEMP_HEADS * HEAD), BF16),
        ],
        scratch_shapes=[
            pltpu.VMEM(spatial_shape, BF16),
            pltpu.VMEM((rows, 3 * TEMP_HEADS * HEAD), BF16),
            pair,
            pair,
        ],
        compiler_params=pltpu.CompilerParams(vmem_limit_bytes=VMEM),
        cost_estimate=moved(6 << 20),
        name="pack_rest",
    )(head_kind, order, queries, keys, values)
    sq = swap(sq)
    tm = lax.all_to_all(tm, "frame", 0, 0, tiled=True)

    blocks = spatial_mask.shape[1]
    same = jnp.eye(blocks, dtype=jnp.bool_)[None]
    bias = jnp.where((jnp.swapaxes(spatial_mask, 1, 2) == 1) | same, 0.0, NEG).astype(F32)
    bias = jnp.pad(bias, ((0, 0), (0, 0), (0, HEAD - blocks)), constant_values=1.0)
    alike = jnp.eye(FRAMES, dtype=jnp.bool_)[None]
    seen = (jnp.swapaxes(temporal_mask, 1, 2) == 1) & (frame_valid[None, :, None] == 1)
    time_bias = jnp.where(seen | alike, 0.0, NEG).astype(F32)
    time_bias = jnp.pad(time_bias, ((0, 0), (0, 0), (0, HEAD - FRAMES)))

    whole = tuple(range(RING))
    half = RING // 2
    right, left = shift(kv, 1), shift(kv, RING - 1)
    marked, state = attention(order, where, bias, [(0, whole)], [kv], queries=sq)
    right2, left2 = shift(right[:half], 1), shift(left[half:], RING - 1)
    near = [(RING - 1, whole), (1, whole)]
    far = [(2, whole[:half]), (2, whole[half:])]
    state = attention(order, where, bias, near, [right, left], carried=(marked, state))
    everything = ([(0, whole)] + near + far, [kv, right, left, right2, left2])
    spatial = attention(
        order, where, bias, far, [right2, left2], carried=(marked, state), everything=everything
    )
    time_out = time_attention(order, time_bias, tm)
    time_out = lax.all_to_all(time_out, "frame", 0, 0, tiled=True)
    out_shape = jax.ShapeDtypeStruct((rows, width), BF16)
    base = pl.pallas_call(
        place_temporal,
        in_specs=[SMEM, ANY],
        out_specs=ANY,
        out_shape=out_shape,
        scratch_shapes=[pltpu.VMEM(time_shape, BF16), dma, dma],
        compiler_params=pltpu.CompilerParams(vmem_limit_bytes=VMEM),
        cost_estimate=moved(2 << 20),
        name="place_temporal",
    )(head_kind, time_out)
    spatial = swap(spatial)
    result = pl.pallas_call(
        place_spatial,
        in_specs=[SMEM, ANY, ANY],
        out_specs=ANY,
        out_shape=out_shape,
        scratch_shapes=[pltpu.VMEM(spatial_shape, BF16), dma, dma],
        compiler_params=pltpu.CompilerParams(vmem_limit_bytes=VMEM),
        input_output_aliases={2: 0},
        cost_estimate=moved(2 << 20),
        name="place_spatial",
    )(head_kind, spatial, base)
    return result[None]


def solution(mesh):
    wide = P("frame", "region", None)
    return jax.shard_map(
        shards,
        mesh=mesh,
        in_specs=(wide, wide, wide, P(), P(), P(), P()),
        out_specs=wide,
        check_vma=False,
    )
```

```python
import functools

import jax
import jax.numpy as jnp
from jax import lax
from jax.experimental import pallas as pl
from jax.experimental.pallas import tpu as pltpu
from jax.sharding import PartitionSpec as P

HEADS = 24
TEMP_HEADS = 12
SPAT_HEADS = HEADS - TEMP_HEADS
BLK = 128
HEAD = 128
RING = 4
GROUP = SPAT_HEADS // RING
FRAMES = 8
BLOCKS = 32
ROWS = 256
TOKENS = RING * ROWS
HALVES = ROWS // BLK
PART = ROWS // FRAMES
TIME_STEP = 6
NEG = -1e30
LEVEL = BLOCKS
LARGE = 2.0**100
LOG2_SCALE = 1.4426950408889634 / HEAD**0.5
AXES = ("frame", "region")
BF16 = jnp.bfloat16
F32 = jnp.float32
ANY = pl.BlockSpec(memory_space=pl.ANY)
SMEM = pl.BlockSpec(memory_space=pltpu.SMEM)
VMEM = pl.BlockSpec(memory_space=pltpu.VMEM)
PARAMS = pltpu.CompilerParams(vmem_limit_bytes=63 * 1024 * 1024)
DMA = pltpu.SemaphoreType.DMA
DMAS = pltpu.SemaphoreType.DMA((RING,))


def flat(y, core, z, x):
    return ((y * 2 + core) * RING + z) * RING + x


def axis_groups(first):
    groups = []
    for y in range(RING):
        for core in range(2):
            along_x = (core == 0) == first
            for other in range(RING):
                groups.append([
                    flat(y, core, other, i) if along_x else flat(y, core, i, other)
                    for i in range(RING)
                ])
    return groups


def shift(tensor, step, first):
    pairs = []
    for group in axis_groups(first):
        for i in range(RING):
            pairs.append((group[i], group[(i + step) % RING]))
    return lax.ppermute(tensor, AXES, sorted(pairs))


def columns(index):
    return pl.ds(pl.multiple_of(index * HEAD, HEAD), HEAD)


def slot_of(own, rank):
    return lax.rem(rank // GROUP - own + RING, RING)


def pack_spatial(kind, q_ref, k_ref, v_ref, *refs):
    outs, (order, where, held, sem_in, sem_out) = refs[:RING], refs[RING:]
    core = lax.rem(lax.axis_index("frame"), 2)
    region = lax.axis_index("region")
    place_z, place_x = region // RING, lax.rem(region, RING)
    own = jnp.where(core == 0, place_x, place_z)
    where[0] = core
    where[1] = jnp.where(core == 0, place_z, place_x)
    where[2] = own
    spatial = jnp.int32(0)
    temporal = jnp.int32(0)
    for head in range(HEADS):
        one = kind[head]

        @pl.when(one == 0)
        def _(spatial=spatial, head=head):
            slot, place = slot_of(own, spatial), lax.rem(spatial, GROUP)
            for which, ref in enumerate((q_ref, k_ref, v_ref)):
                pltpu.make_async_copy(
                    ref.at[:, pl.ds(head * HEAD, HEAD)],
                    held.at[slot, which, place],
                    sem_in.at[slot],
                ).start()

        order[jnp.where(one == 1, SPAT_HEADS + temporal, spatial)] = head
        spatial += 1 - one
        temporal += one
    copies = []
    for slot in (1, 3, 2, 0):
        pltpu.make_async_copy(held.at[slot], held.at[slot], sem_in.at[slot]).wait()
        copies.append(pltpu.make_async_copy(held.at[slot], outs[slot], sem_out.at[slot]))
        copies[-1].start()
    for copy in copies:
        copy.wait()


def pack_temporal(order, q_ref, k_ref, v_ref, out_ref, held, sem_in, sem_out):
    wide = TEMP_HEADS * HEAD
    copies = []
    for which, ref in enumerate((q_ref, k_ref, v_ref)):
        for place in range(TEMP_HEADS):
            pltpu.make_async_copy(
                ref.at[:, columns(order[SPAT_HEADS + place])],
                held.at[:, pl.ds(which * wide + place * HEAD, HEAD)],
                sem_in.at[which],
            ).start()
    for which in range(3):
        part = held.at[:, pl.ds(which * wide, wide)]
        pltpu.make_async_copy(part, part, sem_in.at[which]).wait()
        copies.append(
            pltpu.make_async_copy(part, out_ref.at[:, pl.ds(which * wide, wide)], sem_out.at[which])
        )
        copies[-1].start()
    for copy in copies:
        copy.wait()


def join(*refs):
    k_out, v_out = refs[2 * RING:]
    for slot in range(RING):
        rows = pl.ds(slot * ROWS, ROWS)
        k_out[0, rows, :] = refs[2 * slot][0, 0]
        v_out[0, :, rows] = refs[2 * slot + 1][0, 0].T


def place_first(order, where, time_ref, own_ref, out_ref, held, sem_in, sem_out):
    own = pltpu.make_async_copy(own_ref, held, sem_in)
    own.start()
    for place in range(TEMP_HEADS):
        pltpu.make_async_copy(
            time_ref.at[:, pl.ds(place * HEAD, HEAD)],
            out_ref.at[:, columns(order[SPAT_HEADS + place])],
            sem_out.at[0],
        ).start()
    own.wait()
    place_group(order, where, 0, held, out_ref, sem_out.at[1])
    pltpu.make_async_copy(time_ref, time_ref, sem_out.at[0]).wait()
    pltpu.make_async_copy(held, held, sem_out.at[1]).wait()


def place_group(order, where, slot, held, out_ref, sem):
    group = lax.rem(where[2] + slot, RING)
    for place in range(GROUP):
        pltpu.make_async_copy(
            held.at[place], out_ref.at[:, columns(order[group * GROUP + place])], sem
        ).start()


def place_rest(order, where, *refs):
    count = RING - 1
    parts, (_, out_ref, held, sem_in, sem_out) = refs[:count], refs[count:]
    copies = [
        pltpu.make_async_copy(parts[i], held.at[i], sem_in.at[i]) for i in range(count)
    ]
    for copy in copies:
        copy.start()
    for i, copy in enumerate(copies):
        copy.wait()
        place_group(order, where, i + 1, held.at[i], out_ref, sem_out)
    pltpu.make_async_copy(held, held, sem_out).wait()


def first_block(where, slot, offset):
    place = lax.rem(where[2] - slot + RING, RING)
    ring = lax.rem(where[1] + offset, RING)
    return jnp.where(where[0] == 0, ring * RING + place, place * RING + ring) * HALVES


def mark_queries(where, mask_ref, q_refs, keys, marked_ref):
    lane = lax.broadcasted_iota(jnp.int32, (1, BLOCKS), 1)
    wide = lax.broadcasted_iota(jnp.int32, (BLK, HEAD), 1)
    for slot in range(RING):
        for half in range(HALVES):
            block = first_block(where, slot, 0) + half
            line = mask_ref[0, pl.ds(block, 1), :]
            line = jnp.where((line == 1) | (lane == block), 0.0, NEG)
            line = jnp.concatenate([line, jnp.zeros((1, HEAD - BLOCKS), F32)], axis=1)
            rows = pl.ds(slot * ROWS + half * BLK, BLK)
            query = q_refs[slot][0, 0, half * BLK:(half + 1) * BLK, :]
            level = jnp.sum(
                query.astype(F32) * keys[0, rows, :].astype(F32), axis=1, keepdims=True
            )
            mark = jnp.where(wide == LEVEL, -level, jnp.broadcast_to(line, (BLK, HEAD)))
            marked_ref[0, rows, :HEAD] = query
            marked_ref[0, rows, HEAD:] = mark.astype(BF16)


def mark_keys(where, offset, marks):
    lane = lax.broadcasted_iota(jnp.int32, (ROWS, HEAD), 1)
    half = lax.broadcasted_iota(jnp.int32, (ROWS, HEAD), 0) // BLK
    for slot in range(RING):
        block = first_block(where, slot, offset) + half
        mark = jnp.where((lane == block) | (lane == LEVEL), 1.0, 0.0)
        marks[slot * ROWS:(slot + 1) * ROWS, :] = mark.astype(BF16)


def attend_again(where, marked_ref, keys_all, vals_all, out_refs, marks, keys, vals, sem):
    head = pl.program_id(0)
    lane = lax.broadcasted_iota(jnp.int32, (TOKENS, 2 * HEAD), 1)
    query = marked_ref[0]
    query = jnp.where(lane == HEAD + LEVEL, jnp.zeros_like(query), query)
    offsets = (0, RING - 1, 1, 2)

    def step(turn, carry):
        top, sums, total = carry
        offset = jnp.int32(0)
        for i in range(RING):
            offset = jnp.where(turn == i, offsets[i], offset)

            @pl.when(turn == i)
            def _(i=i):
                copies = [
                    pltpu.make_async_copy(keys_all[i].at[head], keys, sem.at[0]),
                    pltpu.make_async_copy(vals_all[i].at[head], vals, sem.at[1]),
                ]
                for copy in copies:
                    copy.start()
                for copy in copies:
                    copy.wait()

        mark_keys(where, offset, marks)
        scores = lax.dot_general(
            jnp.concatenate([keys[...], marks[...]], axis=1),
            query,
            (((1,), (1,)), ((), ())),
            preferred_element_type=F32,
        )
        new = jnp.maximum(top, jnp.max(scores, axis=0, keepdims=True))
        weights = jnp.exp2((scores - new) * LOG2_SCALE).astype(BF16)
        decay = jnp.exp2((top - new) * LOG2_SCALE)
        sums = sums * decay + jnp.sum(weights.astype(F32), axis=0, keepdims=True)
        total = total * decay + jnp.dot(vals[...], weights, preferred_element_type=F32)
        return new, sums, total

    start = (
        jnp.full((1, TOKENS), -3e38, F32),
        jnp.zeros((1, TOKENS), F32),
        jnp.zeros((HEAD, TOKENS), F32),
    )
    _, sums, total = lax.fori_loop(0, RING, step, start)
    result = total / sums
    for slot in range(RING):
        out_refs[slot][0] = result[:, slot * ROWS:(slot + 1) * ROWS].T.astype(BF16)


def attend(offsets, order, where, *refs):
    count = len(offsets)
    first, last = offsets == (0,), offsets == (2,)
    key_refs, val_refs, refs = refs[:count], refs[count:2 * count], refs[2 * count:]
    if first:
        mask_ref, q_refs, refs = refs[0], refs[1:1 + RING], refs[1 + RING:]
        marked_ref, state_ref, marks = refs
        mark_queries(where, mask_ref, q_refs, key_refs[0], marked_ref)
        state = jnp.zeros((HEAD + 8, TOKENS), F32)
    else:
        marked_ref, before_ref, refs = refs[0], refs[1], refs[2:]
        state = before_ref[0]
        if last:
            keys_all, vals_all, refs = refs[:RING], refs[RING:2 * RING], refs[2 * RING:]
            out_refs, (marks, marks_more, keys, vals, sem) = refs[:RING], refs[RING:]
        else:
            state_ref, marks = refs

    @pl.when(pl.program_id(0) == 0)
    def _():
        for i, offset in enumerate(offsets):
            mark_keys(where, offset, marks.at[pl.ds(i * TOKENS, TOKENS)])

    ones = jnp.ones((8, TOKENS), BF16)
    for i in range(count):
        scores = lax.dot_general(
            jnp.concatenate([key_refs[i][0], marks[i * TOKENS:(i + 1) * TOKENS]], axis=1),
            marked_ref[0],
            (((1,), (1,)), ((), ())),
            preferred_element_type=F32,
        )
        weights = jnp.exp2(scores * LOG2_SCALE).astype(BF16)
        state += jnp.dot(
            jnp.concatenate([val_refs[i][0], ones], axis=0),
            weights,
            preferred_element_type=F32,
        )
    if not last:
        state_ref[0] = state
        return
    sums = state[HEAD:HEAD + 1]
    result = state[:HEAD] / sums
    for slot in range(RING):
        out_refs[slot][0] = result[:, slot * ROWS:(slot + 1) * ROWS].T.astype(BF16)
    fine = jnp.max(jnp.where(sums < LARGE, 0.0, 1.0)) == 0.0

    @pl.when(jnp.logical_not(fine))
    def _():
        attend_again(
            where, marked_ref, keys_all, vals_all, out_refs, marks_more, keys, vals, sem
        )


def attention(offsets, order, where, keys, vals, mask=None, queries=(), carried=(), every=()):
    def at(*block):
        zeros = (0,) * (len(block) - 1)
        return pl.BlockSpec(block, lambda h, o, w: (h,) + zeros)

    count = len(offsets)
    slot_spec = at(1, ROWS, HEAD)
    marked_spec, state_spec = at(1, TOKENS, 2 * HEAD), at(1, HEAD + 8, TOKENS)
    in_specs = [at(1, TOKENS, HEAD)] * count + [at(1, HEAD, TOKENS)] * count
    marked_shape = jax.ShapeDtypeStruct((GROUP, TOKENS, 2 * HEAD), BF16)
    state_shape = jax.ShapeDtypeStruct((GROUP, HEAD + 8, TOKENS), F32)
    scratch = [pltpu.VMEM((count * TOKENS, HEAD), BF16)]
    extra = []
    if queries:
        extra = [mask]
        in_specs += [
            pl.BlockSpec((1, BLOCKS, BLOCKS), lambda h, o, w: (o[w[2] * GROUP + h], 0, 0))
        ]
        in_specs += [
            pl.BlockSpec((1, 1, ROWS, HEAD), lambda h, o, w: (0, h, 0, 0))
        ] * RING
        out_specs, out_shape = [marked_spec, state_spec], [marked_shape, state_shape]
    else:
        in_specs += [marked_spec, state_spec]
        out_specs, out_shape = state_spec, state_shape
    if every:
        in_specs += [ANY] * len(every)
        out_specs = [slot_spec] * RING
        out_shape = [jax.ShapeDtypeStruct((GROUP, ROWS, HEAD), BF16)] * RING
        scratch += [pltpu.VMEM((TOKENS, HEAD), BF16)] * 2
        scratch += [pltpu.VMEM((HEAD, TOKENS), BF16), pltpu.SemaphoreType.DMA((2,))]
    flops = 8 * GROUP * TOKENS * count * TOKENS * HEAD
    return pl.pallas_call(
        functools.partial(attend, offsets),
        grid_spec=pltpu.PrefetchScalarGridSpec(
            num_scalar_prefetch=2,
            grid=(GROUP,),
            in_specs=in_specs,
            out_specs=out_specs,
            scratch_shapes=scratch,
        ),
        out_shape=out_shape,
        compiler_params=PARAMS,
        cost_estimate=pl.CostEstimate(flops=flops, bytes_accessed=4 << 20, transcendentals=0),
        name="spatial_attention",
    )(order, where, *keys, *vals, *extra, *queries, *carried, *every)


def attend_time(order, mask_ref, valid_ref, q_ref, k_ref, v_ref, out_ref):
    lane = lax.broadcasted_iota(jnp.int32, (ROWS, HEAD), 1)
    row = lax.broadcasted_iota(jnp.int32, (ROWS, HEAD), 0)
    frame, place = row // PART, row % PART
    here = lane == FRAMES + place
    inside = (lane >= FRAMES) & (lane < FRAMES + PART)
    key_mark = jnp.where(lane == frame, 1.0, jnp.where(inside & ~here, NEG, 0.0)).astype(BF16)
    ones = jnp.ones((ROWS, HEAD), BF16)
    short = lax.broadcasted_iota(jnp.int32, (FRAMES, FRAMES), 1)
    same = short == lax.broadcasted_iota(jnp.int32, (FRAMES, FRAMES), 0)
    every = range(TIME_STEP)
    at = [slice(slot * HEAD, (slot + 1) * HEAD) for slot in every]
    scores = []
    for slot in every:
        head = order[SPAT_HEADS + pl.program_id(0) * TIME_STEP + slot]
        seen = (mask_ref[head] == 1) & (valid_ref[...] == 1)
        pairs = jnp.where(seen | same, 0.0, NEG)
        pairs = jnp.concatenate([pairs, jnp.zeros((FRAMES, HEAD - FRAMES), F32)], axis=1)
        pairs = jnp.broadcast_to(pairs[:, None, :], (FRAMES, PART, HEAD)).reshape(ROWS, HEAD)
        mark = jnp.where(here, 1.0, pairs).astype(BF16)
        query = jnp.concatenate([q_ref[:, at[slot]], mark], axis=1)
        keys = jnp.concatenate([k_ref[:, at[slot]], key_mark], axis=1)
        scores.append(
            lax.dot_general(query, keys, (((1,), (1,)), ((), ())), preferred_element_type=F32)
        )
    tops = [jnp.max(scores[slot], axis=1, keepdims=True) for slot in every]
    weights = [
        jnp.exp2((scores[slot] - tops[slot]) * LOG2_SCALE).astype(BF16) for slot in every
    ]
    for slot in every:
        vals = jnp.concatenate([v_ref[:, at[slot]], ones], axis=1)
        both = jnp.dot(weights[slot], vals, preferred_element_type=F32)
        out_ref[:, at[slot]] = (both[:, :HEAD] / both[:, HEAD:]).astype(BF16)


def time_attention(order, mask, valid, gathered):
    steps = TEMP_HEADS // TIME_STEP

    def at(which):
        return pl.BlockSpec((ROWS, TIME_STEP * HEAD), lambda h, o: (0, which * steps + h))

    return pl.pallas_call(
        attend_time,
        grid_spec=pltpu.PrefetchScalarGridSpec(
            num_scalar_prefetch=1,
            grid=(steps,),
            in_specs=[
                pl.BlockSpec(mask.shape, lambda h, o: (0, 0, 0)),
                pl.BlockSpec(valid.shape, lambda h, o: (0, 0)),
            ]
            + [at(which) for which in range(3)],
            out_specs=at(0),
        ),
        out_shape=jax.ShapeDtypeStruct((ROWS, TEMP_HEADS * HEAD), BF16),
        compiler_params=PARAMS,
        cost_estimate=pl.CostEstimate(flops=3 << 30, bytes_accessed=4 << 20, transcendentals=0),
        name="temporal_attention",
    )(order, mask, valid, gathered, gathered, gathered)


def call(body, name, moved, in_specs, out_specs, out_shape, scratch, *args, **more):
    return pl.pallas_call(
        body,
        in_specs=in_specs,
        out_specs=out_specs,
        out_shape=out_shape,
        scratch_shapes=scratch,
        compiler_params=PARAMS,
        cost_estimate=pl.CostEstimate(flops=0, bytes_accessed=moved << 20, transcendentals=0),
        name=name,
        **more,
    )(*args)


def shards(queries, keys, values, head_kind, spatial_mask, temporal_mask, frame_valid):
    rows, width = queries.shape[1:]
    queries, keys, values = (t.reshape(rows, width) for t in (queries, keys, values))
    slot_shape = (GROUP, ROWS, HEAD)
    three_shape = (3,) + slot_shape
    wide_shape = (ROWS, 3 * TEMP_HEADS * HEAD)
    *threes, order, where = call(
        pack_spatial,
        "pack_spatial",
        5,
        [SMEM, ANY, ANY, ANY],
        [ANY] * RING + [SMEM] * 2,
        [jax.ShapeDtypeStruct(three_shape, BF16)] * RING
        + [jax.ShapeDtypeStruct((HEADS,), jnp.int32), jax.ShapeDtypeStruct((3,), jnp.int32)],
        [pltpu.VMEM((RING,) + three_shape, BF16), DMAS, DMAS],
        head_kind, queries, keys, values,
    )
    threes = [threes[0]] + [shift(threes[s], s, True) for s in range(1, RING)]
    packed = call(
        pack_temporal,
        "pack_temporal",
        5,
        [SMEM] + [ANY] * 3,
        ANY,
        jax.ShapeDtypeStruct(wide_shape, BF16),
        [pltpu.VMEM(wide_shape, BF16), DMAS, DMAS],
        order, queries, keys, values,
    )
    gathered = lax.all_to_all(packed, "frame", 0, 0, tiled=True)

    def head_block(*block):
        return pl.BlockSpec((1,) + block, lambda h: (h, 0, 0))

    own_keys, own_vals = pl.pallas_call(
        join,
        grid=(GROUP,),
        in_specs=[
            pl.BlockSpec((1, 1, ROWS, HEAD), lambda h, i=i: (i, h, 0, 0))
            for _ in range(RING)
            for i in (1, 2)
        ],
        out_specs=[head_block(TOKENS, HEAD), head_block(HEAD, TOKENS)],
        out_shape=[
            jax.ShapeDtypeStruct((GROUP, TOKENS, HEAD), BF16),
            jax.ShapeDtypeStruct((GROUP, HEAD, TOKENS), BF16),
        ],
        compiler_params=PARAMS,
        cost_estimate=pl.CostEstimate(flops=0, bytes_accessed=3 << 20, transcendentals=0),
        name="join",
    )(*[three for three in threes for _ in range(2)])
    left_keys = shift(own_keys, 1, False)
    right_vals = shift(own_vals, RING - 1, False)
    left_vals = shift(own_vals, 1, False)
    right_keys = shift(own_keys, RING - 1, False)
    carried = attention(
        (0,), order, where, [own_keys], [own_vals], mask=spatial_mask, queries=threes
    )
    far_keys = shift(left_keys, 1, False)
    far_vals = shift(right_vals, RING - 1, False)
    marked, state = carried
    state = attention(
        (RING - 1, 1), order, where, [left_keys, right_keys], [left_vals, right_vals],
        carried=(marked, state),
    )
    every = [own_keys, left_keys, right_keys, far_keys, own_vals, left_vals, right_vals, far_vals]
    parts = attention(
        (2,), order, where, [far_keys], [far_vals], carried=(marked, state), every=every
    )
    parts = [parts[0]] + [shift(parts[s], RING - s, True) for s in range(1, RING)]

    time_out = time_attention(order, temporal_mask, frame_valid[None], gathered)
    time_out = lax.all_to_all(time_out, "frame", 0, 0, tiled=True)
    out_shape = jax.ShapeDtypeStruct((rows, width), BF16)
    base = call(
        place_first,
        "place_first",
        3,
        [SMEM, SMEM, VMEM, ANY],
        ANY,
        out_shape,
        [pltpu.VMEM(slot_shape, BF16), DMA, DMAS],
        order, where, time_out, parts[0],
    )
    result = call(
        place_rest,
        "place_rest",
        1,
        [SMEM, SMEM] + [ANY] * RING,
        ANY,
        out_shape,
        [pltpu.VMEM((RING - 1,) + slot_shape, BF16), DMAS, DMA],
        order, where, *parts[1:], base,
        input_output_aliases={1 + RING: 0},
    )
    return result[None]


def solution(mesh):
    wide = P("frame", "region", None)
    return jax.shard_map(
        shards,
        mesh=mesh,
        in_specs=(wide, wide, wide, P(), P(), P(), P()),
        out_specs=wide,
        check_vma=False,
    )
```

```python
import functools

import jax
import jax.numpy as jnp
from jax import lax
from jax.experimental import pallas as pl
from jax.experimental.pallas import tpu as pltpu
from jax.sharding import PartitionSpec as P

HEADS = 24
TEMP_HEADS = 12
SPAT_HEADS = HEADS - TEMP_HEADS
BLK = 128
HEAD = 128
RING = 4
GROUP = SPAT_HEADS // RING
FRAMES = 8
BLOCKS = 32
ROWS = 256
TOKENS = RING * ROWS
HALVES = ROWS // BLK
PART = ROWS // FRAMES
TIME_STEP = 6
HALF = TOKENS // 2
H0 = 2
H1 = 3
NEG = -1e30
LEVEL = BLOCKS
LARGE = 2.0**100
LOG2_SCALE = 1.4426950408889634 / HEAD**0.5
AXES = ("frame", "region")
BF16 = jnp.bfloat16
F32 = jnp.float32
HBM = pl.BlockSpec(memory_space=pltpu.HBM)
SMEM = pl.BlockSpec(memory_space=pltpu.SMEM)
VMEM = pl.BlockSpec(memory_space=pltpu.VMEM)
PARAMS = pltpu.CompilerParams(vmem_limit_bytes=63 * 1024 * 1024)
DMA = pltpu.SemaphoreType.DMA
DMAS = pltpu.SemaphoreType.DMA((RING,))


def flat(y, core, z, x):
    return ((y * 2 + core) * RING + z) * RING + x


def axis_groups(first):
    groups = []
    for y in range(RING):
        for core in range(2):
            along_x = (core == 0) == first
            for other in range(RING):
                groups.append([
                    flat(y, core, other, i) if along_x else flat(y, core, i, other)
                    for i in range(RING)
                ])
    return groups


def shift(tensor, step, first):
    pairs = []
    for group in axis_groups(first):
        for i in range(RING):
            pairs.append((group[i], group[(i + step) % RING]))
    return lax.ppermute(tensor, AXES, sorted(pairs))


def columns(index):
    return pl.ds(pl.multiple_of(index * HEAD, HEAD), HEAD)


def slot_of(own, rank):
    return lax.rem(rank // GROUP - own + RING, RING)


def pack_spatial(kind, q_ref, k_ref, v_ref, *refs):
    outs, (order, where, held, sem_in, sem_out) = refs[:RING], refs[RING:]
    core = lax.rem(lax.axis_index("frame"), 2)
    region = lax.axis_index("region")
    place_z, place_x = region // RING, lax.rem(region, RING)
    own = jnp.where(core == 0, place_x, place_z)
    where[0] = core
    where[1] = jnp.where(core == 0, place_z, place_x)
    where[2] = own
    spatial = jnp.int32(0)
    temporal = jnp.int32(0)
    for head in range(HEADS):
        one = kind[head]

        @pl.when(one == 0)
        def _(spatial=spatial, head=head):
            slot, place = slot_of(own, spatial), lax.rem(spatial, GROUP)
            for which, ref in enumerate((q_ref, k_ref, v_ref)):
                pltpu.make_async_copy(
                    ref.at[:, pl.ds(head * HEAD, HEAD)],
                    held.at[slot, which, place],
                    sem_in.at[slot],
                ).start()

        order[jnp.where(one == 1, SPAT_HEADS + temporal, spatial)] = head
        spatial += 1 - one
        temporal += one
    copies = []
    for slot in (1, 3, 2, 0):
        pltpu.make_async_copy(held.at[slot], held.at[slot], sem_in.at[slot]).wait()
        copies.append(pltpu.make_async_copy(held.at[slot], outs[slot], sem_out.at[slot]))
        copies[-1].start()
    for copy in copies:
        copy.wait()


def pack_temporal(order, q_ref, k_ref, v_ref, out_ref, held, sem_in, sem_out):
    wide = TEMP_HEADS * HEAD
    copies = []
    for which, ref in enumerate((q_ref, k_ref, v_ref)):
        for place in range(TEMP_HEADS):
            pltpu.make_async_copy(
                ref.at[:, columns(order[SPAT_HEADS + place])],
                held.at[:, pl.ds(which * wide + place * HEAD, HEAD)],
                sem_in.at[which],
            ).start()
    for which in range(3):
        part = held.at[:, pl.ds(which * wide, wide)]
        pltpu.make_async_copy(part, part, sem_in.at[which]).wait()
        copies.append(
            pltpu.make_async_copy(part, out_ref.at[:, pl.ds(which * wide, wide)], sem_out.at[which])
        )
        copies[-1].start()
    for copy in copies:
        copy.wait()


def join(*refs):
    threes, outs = refs[:RING], refs[RING:RING + 2]
    held, v_held, sem_k, sem_v, sem_out = refs[RING + 2:]
    copies = []
    for slot in range(RING):
        half, rows = slot // 2, pl.ds(slot % 2 * ROWS, ROWS)
        copies.append((
            pltpu.make_async_copy(threes[slot].at[2], v_held.at[slot], sem_v.at[slot]),
            pltpu.make_async_copy(threes[slot].at[1], held.at[half, :, 0, rows, :], sem_k.at[slot]),
        ))
        copies[-1][0].start()
        copies[-1][1].start()
    sent = []
    for half in range(2):
        for slot in (2 * half, 2 * half + 1):
            copies[slot][0].wait()
            for head in range(GROUP):
                for block in range(0, ROWS, BLK):
                    rows = pl.ds(slot % 2 * ROWS + block, BLK)
                    held[half, head, 1, rows, :] = v_held[slot, head, block:block + BLK, :].T
            copies[slot][1].wait()
        sent.append(pltpu.make_async_copy(held.at[half], outs[half], sem_out.at[half]))
        sent[-1].start()
    for copy in sent:
        copy.wait()


def place_group(order, where, slot, held, out_ref, sem):
    group = lax.rem(where[2] + slot, RING)
    for place in range(GROUP):
        pltpu.make_async_copy(
            held.at[place], out_ref.at[:, columns(order[group * GROUP + place])], sem
        ).start()


def place(order, where, time_ref, *refs):
    parts, (out_ref, time_held, held, sem_time, sem_in, sem_out) = refs[:RING], refs[RING:]
    time = pltpu.make_async_copy(time_ref, time_held, sem_time.at[0])
    copies = [pltpu.make_async_copy(parts[i], held.at[i], sem_in.at[i]) for i in range(RING)]
    time.start()
    for copy in copies:
        copy.start()
    time.wait()
    for place in range(TEMP_HEADS):
        pltpu.make_async_copy(
            time_held.at[:, pl.ds(place * HEAD, HEAD)],
            out_ref.at[:, columns(order[SPAT_HEADS + place])],
            sem_time.at[1],
        ).start()
    for slot, copy in enumerate(copies):
        copy.wait()
        place_group(order, where, slot, held.at[slot], out_ref, sem_out)
    pltpu.make_async_copy(time_held, time_held, sem_time.at[1]).wait()
    pltpu.make_async_copy(held, held, sem_out).wait()


def first_block(where, slot, offset):
    place = lax.rem(where[2] - slot + RING, RING)
    ring = lax.rem(where[1] + offset, RING)
    return jnp.where(where[0] == 0, ring * RING + place, place * RING + ring) * HALVES


def mark_queries(where, mask_ref, q_refs, kv_refs, marked_ref):
    lane = lax.broadcasted_iota(jnp.int32, (1, BLOCKS), 1)
    wide = lax.broadcasted_iota(jnp.int32, (BLK, HEAD), 1)
    for slot in range(RING):
        for half in range(HALVES):
            block = first_block(where, slot, 0) + half
            line = mask_ref[0, pl.ds(block, 1), :]
            line = jnp.where((line == 1) | (lane == block), 0.0, NEG)
            line = jnp.concatenate([line, jnp.zeros((1, HEAD - BLOCKS), F32)], axis=1)
            rows = pl.ds(slot * ROWS + half * BLK, BLK)
            query = q_refs[slot][0, 0, half * BLK:(half + 1) * BLK, :]
            key = kv_refs[slot // 2][0, 0, pl.ds(slot % 2 * ROWS + half * BLK, BLK), :]
            level = jnp.sum(
                query.astype(F32) * key.astype(F32), axis=1, keepdims=True
            )
            mark = jnp.where(wide == LEVEL, -level, jnp.broadcast_to(line, (BLK, HEAD)))
            marked_ref[0, rows, :HEAD] = query
            marked_ref[0, rows, HEAD:] = mark.astype(BF16)


def mark_keys(where, offset, half, marks):
    lane = lax.broadcasted_iota(jnp.int32, (ROWS, HEAD), 1)
    line = lax.broadcasted_iota(jnp.int32, (ROWS, HEAD), 0) // BLK
    for i in range(2):
        block = first_block(where, 2 * half + i, offset) + line
        mark = jnp.where((lane == block) | (lane == LEVEL), 1.0, 0.0)
        marks[i * ROWS:(i + 1) * ROWS, :] = mark.astype(BF16)


def turned(kv_ref, *lead):
    return jnp.concatenate(
        [kv_ref[(*lead, 1, pl.ds(block, BLK))] for block in range(0, HALF, BLK)], axis=1
    )


def attend_again(where, marked_ref, chunks, kv_all, out_refs, marks, kv, sem):
    head = pl.program_id(0)
    lane = lax.broadcasted_iota(jnp.int32, (TOKENS, 2 * HEAD), 1)
    query = marked_ref[0]
    query = jnp.where(lane == HEAD + LEVEL, jnp.zeros_like(query), query)

    def step(turn, carry):
        top, sums, total = carry
        offset, half = jnp.int32(0), jnp.int32(0)
        for i, (one, other) in enumerate(chunks):
            offset = jnp.where(turn == i, one, offset)
            half = jnp.where(turn == i, other, half)

            @pl.when(turn == i)
            def _(i=i):
                copy = pltpu.make_async_copy(kv_all[i].at[head], kv, sem)
                copy.start()
                copy.wait()

        mark_keys(where, offset, half, marks)
        scores = lax.dot_general(
            jnp.concatenate([kv[0], marks[...]], axis=1),
            query,
            (((1,), (1,)), ((), ())),
            preferred_element_type=F32,
        )
        new = jnp.maximum(top, jnp.max(scores, axis=0, keepdims=True))
        weights = jnp.exp2((scores - new) * LOG2_SCALE).astype(BF16)
        decay = jnp.exp2((top - new) * LOG2_SCALE)
        sums = sums * decay + jnp.sum(weights.astype(F32), axis=0, keepdims=True)
        total = total * decay + jnp.dot(turned(kv), weights, preferred_element_type=F32)
        return new, sums, total

    start = (
        jnp.full((1, TOKENS), -3e38, F32),
        jnp.zeros((1, TOKENS), F32),
        jnp.zeros((HEAD, TOKENS), F32),
    )
    _, sums, total = lax.fori_loop(0, len(chunks), step, start)
    result = total / sums
    for slot in range(RING):
        out_refs[slot][0] = result[:, slot * ROWS:(slot + 1) * ROWS].T.astype(BF16)


def attend(chunks, everything, order, where, *refs):
    count = len(chunks)
    first, last = chunks[0][0] == 0, everything is not None
    kv_refs, refs = refs[:count], refs[count:]
    if first:
        mask_ref, q_refs, refs = refs[0], refs[1:1 + RING], refs[1 + RING:]
        marked_ref, state_ref, marks = refs
        mark_queries(where, mask_ref, q_refs, kv_refs, marked_ref)
        state = jnp.zeros((HEAD + 8, TOKENS), F32)
    else:
        marked_ref, before_ref, refs = refs[0], refs[1], refs[2:]
        state = before_ref[0]
        if last:
            kv_all, refs = refs[:len(everything)], refs[len(everything):]
            out_refs, (marks, marks_more, kv, sem) = refs[:RING], refs[RING:]
        else:
            state_ref, marks = refs

    @pl.when(pl.program_id(0) == 0)
    def _():
        for i, (offset, half) in enumerate(chunks):
            mark_keys(where, offset, half, marks.at[pl.ds(i * HALF, HALF)])

    ones = jnp.ones((8, TOKENS), BF16)
    for i in range(0, count, 2):
        pair = kv_refs[i:i + 2]
        keys = jnp.concatenate([kv_ref[0, 0] for kv_ref in pair], axis=0)
        vals = jnp.concatenate([turned(kv_ref, 0) for kv_ref in pair], axis=1)
        scores = lax.dot_general(
            jnp.concatenate([keys, marks[i * HALF:(i + 2) * HALF]], axis=1),
            marked_ref[0],
            (((1,), (1,)), ((), ())),
            preferred_element_type=F32,
        )
        weights = jnp.exp2(scores * LOG2_SCALE).astype(BF16)
        state += jnp.dot(
            jnp.concatenate([vals, ones], axis=0), weights, preferred_element_type=F32
        )
    if not last:
        state_ref[0] = state
        return
    sums = state[HEAD:HEAD + 1]
    result = state[:HEAD] / sums
    for slot in range(RING):
        out_refs[slot][0] = result[:, slot * ROWS:(slot + 1) * ROWS].T.astype(BF16)
    fine = jnp.max(jnp.where(sums < LARGE, 0.0, 1.0)) == 0.0

    @pl.when(jnp.logical_not(fine))
    def _():
        attend_again(where, marked_ref, everything, kv_all, out_refs, marks_more, kv, sem)


def attention(held, chunks, order, where, mask=None, queries=(), carried=(), everything=None):
    def at(*block):
        zeros = (0,) * (len(block) - 1)
        return pl.BlockSpec(block, lambda h, o, w: (h,) + zeros)

    count = len(chunks)
    slot_spec = at(1, ROWS, HEAD)
    marked_spec, state_spec = at(1, TOKENS, 2 * HEAD), at(1, HEAD + 8, TOKENS)
    in_specs = [at(1, 2, HALF, HEAD)] * count
    marked_shape = jax.ShapeDtypeStruct((GROUP, TOKENS, 2 * HEAD), BF16)
    state_shape = jax.ShapeDtypeStruct((GROUP, HEAD + 8, TOKENS), F32)
    scratch = [pltpu.VMEM((count * HALF, HEAD), BF16)]
    extra = []
    if queries:
        extra = [mask]
        in_specs += [
            pl.BlockSpec((1, BLOCKS, BLOCKS), lambda h, o, w: (o[w[2] * GROUP + h], 0, 0))
        ]
        in_specs += [
            pl.BlockSpec((1, 1, ROWS, HEAD), lambda h, o, w: (0, h, 0, 0))
        ] * RING
        out_specs, out_shape = [marked_spec, state_spec], [marked_shape, state_shape]
    else:
        in_specs += [marked_spec, state_spec]
        out_specs, out_shape = state_spec, state_shape
    every = []
    if everything is not None:
        every = [held[chunk] for chunk in everything]
        in_specs += [HBM] * len(every)
        out_specs = [slot_spec] * RING
        out_shape = [jax.ShapeDtypeStruct((GROUP, ROWS, HEAD), BF16)] * RING
        scratch += [pltpu.VMEM((HALF, HEAD), BF16), pltpu.VMEM((2, HALF, HEAD), BF16), DMA]
    flops = (H0 if queries else H1 if everything is None else 1) * 8 * GROUP * TOKENS * count * HALF * HEAD
    return pl.pallas_call(
        functools.partial(attend, chunks, everything),
        grid_spec=pltpu.PrefetchScalarGridSpec(
            num_scalar_prefetch=2,
            grid=(GROUP,),
            in_specs=in_specs,
            out_specs=out_specs,
            scratch_shapes=scratch,
        ),
        out_shape=out_shape,
        compiler_params=PARAMS,
        cost_estimate=pl.CostEstimate(flops=flops, bytes_accessed=4 << 20, transcendentals=0),
        name="spatial_attention",
    )(order, where, *[held[chunk] for chunk in chunks], *extra, *queries, *carried, *every)


def attend_time(order, mask_ref, valid_ref, q_ref, k_ref, v_ref, out_ref):
    lane = lax.broadcasted_iota(jnp.int32, (ROWS, HEAD), 1)
    row = lax.broadcasted_iota(jnp.int32, (ROWS, HEAD), 0)
    frame, place = row // PART, row % PART
    here = lane == FRAMES + place
    inside = (lane >= FRAMES) & (lane < FRAMES + PART)
    key_mark = jnp.where(lane == frame, 1.0, jnp.where(inside & ~here, NEG, 0.0)).astype(BF16)
    ones = jnp.ones((ROWS, HEAD), BF16)
    short = lax.broadcasted_iota(jnp.int32, (FRAMES, FRAMES), 1)
    same = short == lax.broadcasted_iota(jnp.int32, (FRAMES, FRAMES), 0)
    which = lax.broadcasted_iota(jnp.int32, mask_ref.shape, 2)
    every = range(TIME_STEP)
    at = [slice(slot * HEAD, (slot + 1) * HEAD) for slot in every]
    scores = []
    for slot in every:
        head = order[SPAT_HEADS + pl.program_id(0) * TIME_STEP + slot]
        seen = jnp.sum(jnp.where(which == head, mask_ref[...], 0), axis=2)
        seen = (seen == 1) & (valid_ref[...] == 1)
        pairs = jnp.where(seen | same, 0.0, NEG)
        pairs = jnp.concatenate([pairs, jnp.zeros((FRAMES, HEAD - FRAMES), F32)], axis=1)
        pairs = jnp.broadcast_to(pairs[:, None, :], (FRAMES, PART, HEAD)).reshape(ROWS, HEAD)
        mark = jnp.where(here, 1.0, pairs).astype(BF16)
        query = jnp.concatenate([q_ref[:, at[slot]], mark], axis=1)
        keys = jnp.concatenate([k_ref[:, at[slot]], key_mark], axis=1)
        scores.append(
            lax.dot_general(query, keys, (((1,), (1,)), ((), ())), preferred_element_type=F32)
        )
    tops = [jnp.max(scores[slot], axis=1, keepdims=True) for slot in every]
    weights = [
        jnp.exp2((scores[slot] - tops[slot]) * LOG2_SCALE).astype(BF16) for slot in every
    ]
    for slot in every:
        vals = jnp.concatenate([v_ref[:, at[slot]], ones], axis=1)
        both = jnp.dot(weights[slot], vals, preferred_element_type=F32)
        out_ref[:, at[slot]] = (both[:, :HEAD] / both[:, HEAD:]).astype(BF16)


def time_attention(order, mask, valid, gathered):
    steps = TEMP_HEADS // TIME_STEP

    def at(which):
        return pl.BlockSpec((ROWS, TIME_STEP * HEAD), lambda h, o: (0, which * steps + h))

    return pl.pallas_call(
        attend_time,
        grid_spec=pltpu.PrefetchScalarGridSpec(
            num_scalar_prefetch=1,
            grid=(steps,),
            in_specs=[
                pl.BlockSpec(mask.shape, lambda h, o: (0, 0, 0)),
                pl.BlockSpec(valid.shape, lambda h, o: (0, 0)),
            ]
            + [at(which) for which in range(3)],
            out_specs=at(0),
        ),
        out_shape=jax.ShapeDtypeStruct((ROWS, TEMP_HEADS * HEAD), BF16),
        compiler_params=PARAMS,
        cost_estimate=pl.CostEstimate(flops=3 << 30, bytes_accessed=4 << 20, transcendentals=0),
        name="temporal_attention",
    )(order, mask, valid, gathered, gathered, gathered)


def call(body, name, moved, in_specs, out_specs, out_shape, scratch, *args, **more):
    return pl.pallas_call(
        body,
        in_specs=in_specs,
        out_specs=out_specs,
        out_shape=out_shape,
        scratch_shapes=scratch,
        compiler_params=PARAMS,
        cost_estimate=pl.CostEstimate(flops=0, bytes_accessed=moved << 20, transcendentals=0),
        name=name,
        **more,
    )(*args)


def shards(queries, keys, values, head_kind, spatial_mask, temporal_mask, frame_valid):
    rows, width = queries.shape[1:]
    queries, keys, values = (t.reshape(rows, width) for t in (queries, keys, values))
    slot_shape = (GROUP, ROWS, HEAD)
    three_shape = (3,) + slot_shape
    wide_shape = (ROWS, 3 * TEMP_HEADS * HEAD)
    *threes, order, where = call(
        pack_spatial,
        "pack_spatial",
        5,
        [SMEM, HBM, HBM, HBM],
        [HBM] * RING + [SMEM] * 2,
        [jax.ShapeDtypeStruct(three_shape, BF16)] * RING
        + [jax.ShapeDtypeStruct((HEADS,), jnp.int32), jax.ShapeDtypeStruct((3,), jnp.int32)],
        [pltpu.VMEM((RING,) + three_shape, BF16), DMAS, DMAS],
        head_kind, queries, keys, values,
    )
    threes = [threes[0]] + [shift(threes[s], s, True) for s in range(1, RING)]
    packed = call(
        pack_temporal,
        "pack_temporal",
        40,
        [SMEM] + [HBM] * 3,
        HBM,
        jax.ShapeDtypeStruct(wide_shape, BF16),
        [pltpu.VMEM(wide_shape, BF16), DMAS, DMAS],
        order, queries, keys, values,
    )
    gathered = lax.all_to_all(packed, "frame", 0, 0, tiled=True)

    half_shape = (GROUP, 2, HALF, HEAD)
    held = {}
    held[0, 0], held[0, 1] = call(
        join,
        "join",
        3,
        [HBM] * RING,
        [HBM] * 2,
        [jax.ShapeDtypeStruct(half_shape, BF16)] * 2,
        [
            pltpu.VMEM((2,) + half_shape, BF16),
            pltpu.VMEM((RING,) + slot_shape, BF16),
            DMAS,
            DMAS,
            DMAS,
        ],
        *threes,
    )
    left, right, far = RING - 1, 1, 2
    held[left, 0] = shift(held[0, 0], 1, False)
    held[right, 1] = shift(held[0, 1], RING - 1, False)
    held[left, 1] = shift(held[0, 1], 1, False)
    held[right, 0] = shift(held[0, 0], RING - 1, False)
    marked, state = attention(
        held, [(0, 0), (0, 1)], order, where, mask=spatial_mask, queries=threes
    )
    held[far, 0] = shift(held[left, 0], 1, False)
    held[far, 1] = shift(held[right, 1], RING - 1, False)
    state = attention(held, [(left, 0), (right, 1)], order, where, carried=(marked, state))
    parts = attention(
        held,
        [(left, 1), (right, 0), (far, 0), (far, 1)],
        order,
        where,
        carried=(marked, state),
        everything=[(offset, half) for offset in (0, left, right, far) for half in range(2)],
    )
    parts = [parts[0]] + [shift(parts[s], RING - s, True) for s in range(1, RING)]

    time_out = time_attention(order, jnp.transpose(temporal_mask, (1, 2, 0)), frame_valid[None], gathered)
    time_out = lax.all_to_all(time_out, "frame", 0, 0, tiled=True)
    out_shape = jax.ShapeDtypeStruct((rows, width), BF16)
    result = call(
        place,
        "place",
        4,
        [SMEM, SMEM] + [HBM] * (1 + RING),
        HBM,
        out_shape,
        [
            pltpu.VMEM((ROWS, TEMP_HEADS * HEAD), BF16),
            pltpu.VMEM((RING,) + slot_shape, BF16),
            DMAS,
            DMAS,
            DMA,
        ],
        order, where, time_out, *parts,
    )
    return result[None]


def solution(mesh):
    wide = P("frame", "region", None)
    return jax.shard_map(
        shards,
        mesh=mesh,
        in_specs=(wide, wide, wide, P(), P(), P(), P()),
        out_specs=wide,
        check_vma=False,
    )
```

```python
import functools

import jax
import jax.numpy as jnp
from jax import lax
from jax.experimental import pallas as pl
from jax.experimental.pallas import tpu as pltpu
from jax.sharding import PartitionSpec as P

HEADS = 24
TEMP_HEADS = 12
SPAT_HEADS = HEADS - TEMP_HEADS
BLK = 128
HEAD = 128
RING = 4
GROUP = SPAT_HEADS // RING
FRAMES = 8
BLOCKS = 32
ROWS = 256
TOKENS = RING * ROWS
HALVES = ROWS // BLK
PART = ROWS // FRAMES
TIME_STEP = 6
SENT = (1, 3, 2)
FILLER = 114688
HALF = TOKENS // 2
H0 = 2
H1 = 4
NEG = -1e30
LEVEL = BLOCKS
LARGE = 2.0**100
LOG2_SCALE = 1.4426950408889634 / HEAD**0.5
AXES = ("frame", "region")
BF16 = jnp.bfloat16
F32 = jnp.float32
HBM = pl.BlockSpec(memory_space=pltpu.HBM)
SMEM = pl.BlockSpec(memory_space=pltpu.SMEM)
VMEM = pl.BlockSpec(memory_space=pltpu.VMEM)
PARAMS = pltpu.CompilerParams(vmem_limit_bytes=63 * 1024 * 1024)
DMA = pltpu.SemaphoreType.DMA
DMAS = pltpu.SemaphoreType.DMA((RING,))


def flat(y, core, z, x):
    return ((y * 2 + core) * RING + z) * RING + x


def axis_groups(first):
    groups = []
    for y in range(RING):
        for core in range(2):
            along_x = (core == 0) == first
            for other in range(RING):
                groups.append([
                    flat(y, core, other, i) if along_x else flat(y, core, i, other)
                    for i in range(RING)
                ])
    return groups


def shift(tensor, step, first):
    pairs = []
    for group in axis_groups(first):
        for i in range(RING):
            pairs.append((group[i], group[(i + step) % RING]))
    return lax.ppermute(tensor, AXES, sorted(pairs))


def columns(index):
    return pl.ds(pl.multiple_of(index * HEAD, HEAD), HEAD)


def slot_of(own, rank):
    return lax.rem(rank // GROUP - own + RING, RING)


def pack_spatial(kind, q_ref, k_ref, v_ref, *refs):
    outs, (order, where, held, sem_in, sem_out) = refs[:RING - 1], refs[RING - 1:]
    core = lax.rem(lax.axis_index("frame"), 2)
    region = lax.axis_index("region")
    place_z, place_x = region // RING, lax.rem(region, RING)
    own = jnp.where(core == 0, place_x, place_z)
    where[0] = core
    where[1] = jnp.where(core == 0, place_z, place_x)
    where[2] = own
    spatial = jnp.int32(0)
    temporal = jnp.int32(0)
    for head in range(HEADS):
        one = kind[head]
        order[jnp.where(one == 1, SPAT_HEADS + temporal, spatial)] = head
        spatial += 1 - one
        temporal += one
    for slot in SENT:
        fetch_group(order, own, slot, (q_ref, k_ref, v_ref), held.at[slot - 1], sem_in.at[slot])
    copies = []
    for slot in SENT:
        part = held.at[slot - 1]
        pltpu.make_async_copy(part, part, sem_in.at[slot]).wait()
        copies.append(pltpu.make_async_copy(part, outs[slot - 1], sem_out.at[slot]))
        copies[-1].start()
    for copy in copies:
        copy.wait()


def fetch_group(order, own, slot, sources, held, sem):
    group = lax.rem(own + slot, RING)
    for place in range(GROUP):
        head = order[group * GROUP + place]
        for which, ref in enumerate(sources):
            pltpu.make_async_copy(ref.at[:, columns(head)], held.at[which, place], sem).start()


def pack_rest(order, where, q_ref, k_ref, v_ref, own_ref, out_ref, held, wide_held, sem_own, sem_in, sem_out):
    wide = TEMP_HEADS * HEAD
    copies = []
    sources = (q_ref, k_ref, v_ref)
    for which, ref in enumerate(sources):
        for place in range(TEMP_HEADS):
            pltpu.make_async_copy(
                ref.at[:, columns(order[SPAT_HEADS + place])],
                wide_held.at[:, pl.ds(which * wide + place * HEAD, HEAD)],
                sem_in.at[which],
            ).start()
    fetch_group(order, where[2], 0, sources, held, sem_own.at[0])
    for which in range(3):
        part = wide_held.at[:, pl.ds(which * wide, wide)]
        pltpu.make_async_copy(part, part, sem_in.at[which]).wait()
        copies.append(
            pltpu.make_async_copy(part, out_ref.at[:, pl.ds(which * wide, wide)], sem_out.at[which])
        )
        copies[-1].start()
    pltpu.make_async_copy(held, held, sem_own.at[0]).wait()
    copies.append(pltpu.make_async_copy(held, own_ref, sem_own.at[1]))
    copies[-1].start()
    for copy in copies:
        copy.wait()


def join(first_ref, second_ref, out_ref, held, v_held, sem_k, sem_v, sem_out):
    copies = []
    for slot, ref in enumerate((first_ref, second_ref)):
        rows = pl.ds(slot * ROWS, ROWS)
        copies.append((
            pltpu.make_async_copy(ref.at[2], v_held.at[slot], sem_v.at[slot]),
            pltpu.make_async_copy(ref.at[1], held.at[:, 0, rows, :], sem_k.at[slot]),
        ))
        copies[-1][0].start()
        copies[-1][1].start()
    for slot in range(2):
        copies[slot][0].wait()
        for head in range(GROUP):
            for block in range(0, ROWS, BLK):
                rows = pl.ds(slot * ROWS + block, BLK)
                held[head, 1, rows, :] = v_held[slot, head, block:block + BLK, :].T
    for slot in range(2):
        copies[slot][1].wait()
    copy = pltpu.make_async_copy(held, out_ref, sem_out)
    copy.start()
    copy.wait()


def place_group(order, where, slot, held, out_ref, sem):
    group = lax.rem(where[2] + slot, RING)
    for place in range(GROUP):
        pltpu.make_async_copy(
            held.at[place], out_ref.at[:, columns(order[group * GROUP + place])], sem
        ).start()


def place_first(order, where, time_ref, own_ref, out_ref, time_held, held, sem_in, sem_out, _):
    own = pltpu.make_async_copy(own_ref, held, sem_in.at[0])
    time = pltpu.make_async_copy(time_ref, time_held, sem_in.at[1])
    time.start()
    own.start()
    time.wait()
    for place in range(TEMP_HEADS):
        pltpu.make_async_copy(
            time_held.at[:, pl.ds(place * HEAD, HEAD)],
            out_ref.at[:, columns(order[SPAT_HEADS + place])],
            sem_out.at[1],
        ).start()
    own.wait()
    place_group(order, where, 0, held, out_ref, sem_out.at[0])
    pltpu.make_async_copy(time_held, time_held, sem_out.at[1]).wait()
    pltpu.make_async_copy(held, held, sem_out.at[0]).wait()


def place_rest(order, where, *refs):
    count = RING - 1
    parts, (_, out_ref, held, sem_in, sem_out, _) = refs[:count], refs[count:]
    copies = [
        pltpu.make_async_copy(parts[i], held.at[i], sem_in.at[i]) for i in range(count)
    ]
    for copy in copies:
        copy.start()
    for i, copy in enumerate(copies):
        copy.wait()
        place_group(order, where, i + 1, held.at[i], out_ref, sem_out)
    pltpu.make_async_copy(held, held, sem_out).wait()


def first_block(where, slot, offset):
    place = lax.rem(where[2] - slot + RING, RING)
    ring = lax.rem(where[1] + offset, RING)
    return jnp.where(where[0] == 0, ring * RING + place, place * RING + ring) * HALVES


def mark_queries(where, mask_ref, q_refs, kv_refs, marked_ref):
    lane = lax.broadcasted_iota(jnp.int32, (1, BLOCKS), 1)
    wide = lax.broadcasted_iota(jnp.int32, (BLK, HEAD), 1)
    for slot in range(RING):
        for half in range(HALVES):
            block = first_block(where, slot, 0) + half
            line = mask_ref[0, pl.ds(block, 1), :]
            line = jnp.where((line == 1) | (lane == block), 0.0, NEG)
            line = jnp.concatenate([line, jnp.zeros((1, HEAD - BLOCKS), F32)], axis=1)
            rows = pl.ds(slot * ROWS + half * BLK, BLK)
            query = q_refs[slot][0, 0, half * BLK:(half + 1) * BLK, :]
            key = kv_refs[slot // 2][0, 0, pl.ds(slot % 2 * ROWS + half * BLK, BLK), :]
            level = jnp.sum(
                query.astype(F32) * key.astype(F32), axis=1, keepdims=True
            )
            mark = jnp.where(wide == LEVEL, -level, jnp.broadcast_to(line, (BLK, HEAD)))
            marked_ref[0, rows, :HEAD] = query
            marked_ref[0, rows, HEAD:] = mark.astype(BF16)


def mark_keys(where, offset, half, marks):
    lane = lax.broadcasted_iota(jnp.int32, (ROWS, HEAD), 1)
    line = lax.broadcasted_iota(jnp.int32, (ROWS, HEAD), 0) // BLK
    for i in range(2):
        block = first_block(where, 2 * half + i, offset) + line
        mark = jnp.where((lane == block) | (lane == LEVEL), 1.0, 0.0)
        marks[i * ROWS:(i + 1) * ROWS, :] = mark.astype(BF16)


def turned(kv_ref, *lead):
    return jnp.concatenate(
        [kv_ref[(*lead, 1, pl.ds(block, BLK))] for block in range(0, HALF, BLK)], axis=1
    )


def attend_again(where, marked_ref, chunks, kv_all, out_refs, marks, kv, sem):
    head = pl.program_id(0)
    lane = lax.broadcasted_iota(jnp.int32, (TOKENS, 2 * HEAD), 1)
    query = marked_ref[0]
    query = jnp.where(lane == HEAD + LEVEL, jnp.zeros_like(query), query)

    def step(turn, carry):
        top, sums, total = carry
        offset, half = jnp.int32(0), jnp.int32(0)
        for i, (one, other) in enumerate(chunks):
            offset = jnp.where(turn == i, one, offset)
            half = jnp.where(turn == i, other, half)

            @pl.when(turn == i)
            def _(i=i):
                copy = pltpu.make_async_copy(kv_all[i].at[head], kv, sem)
                copy.start()
                copy.wait()

        mark_keys(where, offset, half, marks)
        scores = lax.dot_general(
            jnp.concatenate([kv[0], marks[...]], axis=1),
            query,
            (((1,), (1,)), ((), ())),
            preferred_element_type=F32,
        )
        new = jnp.maximum(top, jnp.max(scores, axis=0, keepdims=True))
        weights = jnp.exp2((scores - new) * LOG2_SCALE).astype(BF16)
        decay = jnp.exp2((top - new) * LOG2_SCALE)
        sums = sums * decay + jnp.sum(weights.astype(F32), axis=0, keepdims=True)
        total = total * decay + jnp.dot(turned(kv), weights, preferred_element_type=F32)
        return new, sums, total

    start = (
        jnp.full((1, TOKENS), -3e38, F32),
        jnp.zeros((1, TOKENS), F32),
        jnp.zeros((HEAD, TOKENS), F32),
    )
    _, sums, total = lax.fori_loop(0, len(chunks), step, start)
    result = total / sums
    for slot in range(RING):
        out_refs[slot][0] = result[:, slot * ROWS:(slot + 1) * ROWS].T.astype(BF16)


def attend(chunks, everything, order, where, *refs):
    count = len(chunks)
    first, last = chunks[0][0] == 0, everything is not None
    kv_refs, refs = refs[:count], refs[count:]
    if first:
        mask_ref, q_refs, refs = refs[0], refs[1:1 + RING], refs[1 + RING:]
        marked_ref, state_ref, marks = refs
        mark_queries(where, mask_ref, q_refs, kv_refs, marked_ref)
        state = jnp.zeros((HEAD + 8, TOKENS), F32)
    else:
        marked_ref, before_ref, refs = refs[0], refs[1], refs[2:]
        state = before_ref[0]
        if last:
            kv_all, refs = refs[:len(everything)], refs[len(everything):]
            out_refs, (marks, marks_more, kv, sem) = refs[:RING], refs[RING:]
        else:
            state_ref, marks = refs

    @pl.when(pl.program_id(0) == 0)
    def _():
        for i, (offset, half) in enumerate(chunks):
            mark_keys(where, offset, half, marks.at[pl.ds(i * HALF, HALF)])

    ones = jnp.ones((8, TOKENS), BF16)
    for i in range(0, count, 2):
        pair = kv_refs[i:i + 2]
        keys = jnp.concatenate([kv_ref[0, 0] for kv_ref in pair], axis=0)
        vals = jnp.concatenate([turned(kv_ref, 0) for kv_ref in pair], axis=1)
        scores = lax.dot_general(
            jnp.concatenate([keys, marks[i * HALF:(i + 2) * HALF]], axis=1),
            marked_ref[0],
            (((1,), (1,)), ((), ())),
            preferred_element_type=F32,
        )
        weights = jnp.exp2(scores * LOG2_SCALE).astype(BF16)
        state += jnp.dot(
            jnp.concatenate([vals, ones], axis=0), weights, preferred_element_type=F32
        )
    if not last:
        state_ref[0] = state
        return
    sums = state[HEAD:HEAD + 1]
    result = state[:HEAD] / sums
    for slot in range(RING):
        out_refs[slot][0] = result[:, slot * ROWS:(slot + 1) * ROWS].T.astype(BF16)
    fine = jnp.max(jnp.where(sums < LARGE, 0.0, 1.0)) == 0.0

    @pl.when(jnp.logical_not(fine))
    def _():
        attend_again(where, marked_ref, everything, kv_all, out_refs, marks_more, kv, sem)


def attention(held, chunks, order, where, mask=None, queries=(), carried=(), everything=None):
    def at(*block):
        zeros = (0,) * (len(block) - 1)
        return pl.BlockSpec(block, lambda h, o, w: (h,) + zeros)

    count = len(chunks)
    slot_spec = at(1, ROWS, HEAD)
    marked_spec, state_spec = at(1, TOKENS, 2 * HEAD), at(1, HEAD + 8, TOKENS)
    in_specs = [at(1, 2, HALF, HEAD)] * count
    marked_shape = jax.ShapeDtypeStruct((GROUP, TOKENS, 2 * HEAD), BF16)
    state_shape = jax.ShapeDtypeStruct((GROUP, HEAD + 8, TOKENS), F32)
    scratch = [pltpu.VMEM((count * HALF, HEAD), BF16)]
    extra = []
    if queries:
        extra = [mask]
        in_specs += [
            pl.BlockSpec((1, BLOCKS, BLOCKS), lambda h, o, w: (o[w[2] * GROUP + h], 0, 0))
        ]
        in_specs += [
            pl.BlockSpec((1, 1, ROWS, HEAD), lambda h, o, w: (0, h, 0, 0))
        ] * RING
        out_specs, out_shape = [marked_spec, state_spec], [marked_shape, state_shape]
    else:
        in_specs += [marked_spec, state_spec]
        out_specs, out_shape = state_spec, state_shape
    every = []
    if everything is not None:
        every = [held[chunk] for chunk in everything]
        in_specs += [HBM] * len(every)
        out_specs = [slot_spec] * RING
        out_shape = [jax.ShapeDtypeStruct((GROUP, ROWS, HEAD), BF16)] * RING
        scratch += [pltpu.VMEM((HALF, HEAD), BF16), pltpu.VMEM((2, HALF, HEAD), BF16), DMA]
    flops = (H0 if queries else H1 if everything is None else 1) * 8 * GROUP * TOKENS * count * HALF * HEAD
    return pl.pallas_call(
        functools.partial(attend, chunks, everything),
        grid_spec=pltpu.PrefetchScalarGridSpec(
            num_scalar_prefetch=2,
            grid=(GROUP,),
            in_specs=in_specs,
            out_specs=out_specs,
            scratch_shapes=scratch,
        ),
        out_shape=out_shape,
        compiler_params=PARAMS,
        cost_estimate=pl.CostEstimate(flops=flops, bytes_accessed=4 << 20, transcendentals=0),
        name="spatial_attention",
    )(order, where, *[held[chunk] for chunk in chunks], *extra, *queries, *carried, *every)


def attend_time(order, mask_ref, valid_ref, q_ref, k_ref, v_ref, out_ref):
    lane = lax.broadcasted_iota(jnp.int32, (ROWS, HEAD), 1)
    row = lax.broadcasted_iota(jnp.int32, (ROWS, HEAD), 0)
    frame, place = row // PART, row % PART
    here = lane == FRAMES + place
    inside = (lane >= FRAMES) & (lane < FRAMES + PART)
    key_mark = jnp.where(lane == frame, 1.0, jnp.where(inside & ~here, NEG, 0.0)).astype(BF16)
    ones = jnp.ones((ROWS, HEAD), BF16)
    short = lax.broadcasted_iota(jnp.int32, (FRAMES, FRAMES), 1)
    same = short == lax.broadcasted_iota(jnp.int32, (FRAMES, FRAMES), 0)
    which = lax.broadcasted_iota(jnp.int32, mask_ref.shape, 2)
    every = range(TIME_STEP)
    at = [slice(slot * HEAD, (slot + 1) * HEAD) for slot in every]
    scores = []
    for slot in every:
        head = order[SPAT_HEADS + pl.program_id(0) * TIME_STEP + slot]
        seen = jnp.sum(jnp.where(which == head, mask_ref[...], 0), axis=2)
        seen = (seen == 1) & (valid_ref[...] == 1)
        pairs = jnp.where(seen | same, 0.0, NEG)
        pairs = jnp.concatenate([pairs, jnp.zeros((FRAMES, HEAD - FRAMES), F32)], axis=1)
        pairs = jnp.broadcast_to(pairs[:, None, :], (FRAMES, PART, HEAD)).reshape(ROWS, HEAD)
        mark = jnp.where(here, 1.0, pairs).astype(BF16)
        query = jnp.concatenate([q_ref[:, at[slot]], mark], axis=1)
        keys = jnp.concatenate([k_ref[:, at[slot]], key_mark], axis=1)
        scores.append(
            lax.dot_general(query, keys, (((1,), (1,)), ((), ())), preferred_element_type=F32)
        )
    tops = [jnp.max(scores[slot], axis=1, keepdims=True) for slot in every]
    weights = [
        jnp.exp2((scores[slot] - tops[slot]) * LOG2_SCALE).astype(BF16) for slot in every
    ]
    for slot in every:
        vals = jnp.concatenate([v_ref[:, at[slot]], ones], axis=1)
        both = jnp.dot(weights[slot], vals, preferred_element_type=F32)
        out_ref[:, at[slot]] = (both[:, :HEAD] / both[:, HEAD:]).astype(BF16)


def time_attention(order, mask, valid, gathered):
    steps = TEMP_HEADS // TIME_STEP

    def at(which):
        return pl.BlockSpec((ROWS, TIME_STEP * HEAD), lambda h, o: (0, which * steps + h))

    return pl.pallas_call(
        attend_time,
        grid_spec=pltpu.PrefetchScalarGridSpec(
            num_scalar_prefetch=1,
            grid=(steps,),
            in_specs=[
                pl.BlockSpec(mask.shape, lambda h, o: (0, 0, 0)),
                pl.BlockSpec(valid.shape, lambda h, o: (0, 0)),
            ]
            + [at(which) for which in range(3)],
            out_specs=at(0),
        ),
        out_shape=jax.ShapeDtypeStruct((ROWS, TEMP_HEADS * HEAD), BF16),
        compiler_params=PARAMS,
        cost_estimate=pl.CostEstimate(flops=3 << 30, bytes_accessed=4 << 20, transcendentals=0),
        name="temporal_attention",
    )(order, mask, valid, gathered, gathered, gathered)


def call(body, name, moved, in_specs, out_specs, out_shape, scratch, *args, **more):
    return pl.pallas_call(
        body,
        in_specs=in_specs,
        out_specs=out_specs,
        out_shape=out_shape,
        scratch_shapes=scratch,
        compiler_params=PARAMS,
        cost_estimate=pl.CostEstimate(flops=0, bytes_accessed=moved << 20, transcendentals=0),
        name=name,
        **more,
    )(*args)


def shards(queries, keys, values, head_kind, spatial_mask, temporal_mask, frame_valid):
    rows, width = queries.shape[1:]
    queries, keys, values = (t.reshape(rows, width) for t in (queries, keys, values))
    slot_shape = (GROUP, ROWS, HEAD)
    three_shape = (3,) + slot_shape
    wide_shape = (ROWS, 3 * TEMP_HEADS * HEAD)
    *threes, order, where = call(
        pack_spatial,
        "pack_spatial",
        5,
        [SMEM, HBM, HBM, HBM],
        [HBM] * (RING - 1) + [SMEM] * 2,
        [jax.ShapeDtypeStruct(three_shape, BF16)] * (RING - 1)
        + [jax.ShapeDtypeStruct((HEADS,), jnp.int32), jax.ShapeDtypeStruct((3,), jnp.int32)],
        [pltpu.VMEM((RING - 1,) + three_shape, BF16), DMAS, DMAS],
        head_kind, queries, keys, values,
    )
    threes = [shift(threes[s - 1], s, True) for s in range(1, RING)]
    own_three, packed = call(
        pack_rest,
        "pack_rest",
        40,
        [SMEM] * 2 + [HBM] * 3,
        [HBM] * 2,
        [jax.ShapeDtypeStruct(three_shape, BF16), jax.ShapeDtypeStruct(wide_shape, BF16)],
        [pltpu.VMEM(three_shape, BF16), pltpu.VMEM(wide_shape, BF16)] + [DMAS] * 3,
        order, where, queries, keys, values,
    )
    threes = [own_three] + threes
    gathered = lax.all_to_all(packed, "frame", 0, 0, tiled=True)

    half_shape = (GROUP, 2, HALF, HEAD)
    held = {}
    for half in range(2):
        held[0, half] = call(
            join,
            "join",
            2,
            [HBM] * 2,
            HBM,
            jax.ShapeDtypeStruct(half_shape, BF16),
            [pltpu.VMEM(half_shape, BF16), pltpu.VMEM((2,) + slot_shape, BF16), DMAS, DMAS, DMA],
            *threes[2 * half:2 * half + 2],
        )
        if half == 0:
            held[0, 0], threes[2], threes[3] = lax.optimization_barrier(
                (held[0, 0], threes[2], threes[3])
            )
    left, right, far = RING - 1, 1, 2
    held[left, 0] = shift(held[0, 0], 1, False)
    held[right, 1] = shift(held[0, 1], RING - 1, False)
    held[left, 1] = shift(held[0, 1], 1, False)
    held[right, 0] = shift(held[0, 0], RING - 1, False)
    marked, state = attention(
        held, [(0, 0), (0, 1)], order, where, mask=spatial_mask, queries=threes
    )
    held[far, 0] = shift(held[left, 0], 1, False)
    held[far, 1] = shift(held[right, 1], RING - 1, False)
    state = attention(held, [(left, 0), (right, 1)], order, where, carried=(marked, state))
    parts = attention(
        held,
        [(left, 1), (right, 0), (far, 0), (far, 1)],
        order,
        where,
        carried=(marked, state),
        everything=[(offset, half) for offset in (0, left, right, far) for half in range(2)],
    )
    parts = [parts[0]] + [shift(parts[s], RING - s, True) for s in range(1, RING)]

    time_out = time_attention(order, jnp.transpose(temporal_mask, (1, 2, 0)), frame_valid[None], gathered)
    time_out = lax.all_to_all(time_out, "frame", 0, 0, tiled=True)
    out_shape = jax.ShapeDtypeStruct((rows, width), BF16)
    room = pltpu.VMEM((FILLER, HEAD), F32)
    base = call(
        place_first,
        "place_first",
        3,
        [SMEM, SMEM, HBM, HBM],
        HBM,
        out_shape,
        [pltpu.VMEM((ROWS, TEMP_HEADS * HEAD), BF16), pltpu.VMEM(slot_shape, BF16), DMAS, DMAS, room],
        order, where, time_out, parts[0],
    )
    result = call(
        place_rest,
        "place_rest",
        1,
        [SMEM, SMEM] + [HBM] * RING,
        HBM,
        out_shape,
        [pltpu.VMEM((RING - 1,) + slot_shape, BF16), DMAS, DMA, room],
        order, where, *parts[1:], base,
        input_output_aliases={1 + RING: 0},
    )
    return result[None]


def solution(mesh):
    wide = P("frame", "region", None)
    return jax.shard_map(
        shards,
        mesh=mesh,
        in_specs=(wide, wide, wide, P(), P(), P(), P()),
        out_specs=wide,
        check_vma=False,
    )
```

```python
import functools

import jax
import jax.numpy as jnp
from jax import lax
from jax.experimental import pallas as pl
from jax.experimental.pallas import tpu as pltpu
from jax.sharding import PartitionSpec as P

HEADS = 24
TEMP_HEADS = 12
SPAT_HEADS = HEADS - TEMP_HEADS
BLK = 128
HEAD = 128
RING = 4
GROUP = SPAT_HEADS // RING
FRAMES = 8
BLOCKS = 32
ROWS = 256
TOKENS = RING * ROWS
HALVES = ROWS // BLK
PART = ROWS // FRAMES
TIME_STEP = 6
SENT = (1, 3, 2)
FILLER = 114688
HALF = TOKENS // 2
H0 = 2
H1 = 4
NEG = -1e30
LEVEL = BLOCKS
LARGE = 2.0**100
LOG2_SCALE = 1.4426950408889634 / HEAD**0.5
AXES = ("frame", "region")
BF16 = jnp.bfloat16
F32 = jnp.float32
HBM = pl.BlockSpec(memory_space=pltpu.HBM)
SMEM = pl.BlockSpec(memory_space=pltpu.SMEM)
VMEM = pl.BlockSpec(memory_space=pltpu.VMEM)
PARAMS = pltpu.CompilerParams(vmem_limit_bytes=63 * 1024 * 1024)
DMA = pltpu.SemaphoreType.DMA
DMAS = pltpu.SemaphoreType.DMA((RING,))


def flat(y, core, z, x):
    return ((y * 2 + core) * RING + z) * RING + x


def axis_groups(first):
    groups = []
    for y in range(RING):
        for core in range(2):
            along_x = (core == 0) == first
            for other in range(RING):
                groups.append([
                    flat(y, core, other, i) if along_x else flat(y, core, i, other)
                    for i in range(RING)
                ])
    return groups


def shift(tensor, step, first):
    pairs = []
    for group in axis_groups(first):
        for i in range(RING):
            pairs.append((group[i], group[(i + step) % RING]))
    return lax.ppermute(tensor, AXES, sorted(pairs))


def columns(index):
    return pl.ds(pl.multiple_of(index * HEAD, HEAD), HEAD)


def slot_of(own, rank):
    return lax.rem(rank // GROUP - own + RING, RING)


def pack_spatial(kind, q_ref, k_ref, v_ref, *refs):
    outs, (order, where, held, sem_in, sem_out) = refs[:RING - 1], refs[RING - 1:]
    core = lax.rem(lax.axis_index("frame"), 2)
    region = lax.axis_index("region")
    place_z, place_x = region // RING, lax.rem(region, RING)
    own = jnp.where(core == 0, place_x, place_z)
    where[0] = core
    where[1] = jnp.where(core == 0, place_z, place_x)
    where[2] = own
    spatial = jnp.int32(0)
    temporal = jnp.int32(0)
    for head in range(HEADS):
        one = kind[head]
        order[jnp.where(one == 1, SPAT_HEADS + temporal, spatial)] = head
        spatial += 1 - one
        temporal += one
    for slot in SENT:
        fetch_group(order, own, slot, (q_ref, k_ref, v_ref), held.at[slot - 1], sem_in.at[slot])
    copies = []
    for slot in SENT:
        part = held.at[slot - 1]
        pltpu.make_async_copy(part, part, sem_in.at[slot]).wait()
        copies.append(pltpu.make_async_copy(part, outs[slot - 1], sem_out.at[slot]))
        copies[-1].start()
    for copy in copies:
        copy.wait()


def fetch_group(order, own, slot, sources, held, sem):
    group = lax.rem(own + slot, RING)
    for place in range(GROUP):
        head = order[group * GROUP + place]
        for which, ref in enumerate(sources):
            pltpu.make_async_copy(ref.at[:, columns(head)], held.at[which, place], sem).start()


def pack_rest(order, where, q_ref, k_ref, v_ref, own_ref, out_ref, held, wide_held, sem_own, sem_in, sem_out):
    wide = TEMP_HEADS * HEAD
    copies = []
    sources = (q_ref, k_ref, v_ref)
    for which, ref in enumerate(sources):
        for place in range(TEMP_HEADS):
            pltpu.make_async_copy(
                ref.at[:, columns(order[SPAT_HEADS + place])],
                wide_held.at[:, pl.ds(which * wide + place * HEAD, HEAD)],
                sem_in.at[which],
            ).start()
    fetch_group(order, where[2], 0, sources, held, sem_own.at[0])
    for which in range(3):
        part = wide_held.at[:, pl.ds(which * wide, wide)]
        pltpu.make_async_copy(part, part, sem_in.at[which]).wait()
        copies.append(
            pltpu.make_async_copy(part, out_ref.at[:, pl.ds(which * wide, wide)], sem_out.at[which])
        )
        copies[-1].start()
    pltpu.make_async_copy(held, held, sem_own.at[0]).wait()
    copies.append(pltpu.make_async_copy(held, own_ref, sem_own.at[1]))
    copies[-1].start()
    for copy in copies:
        copy.wait()


def join(first_ref, second_ref, out_ref, held, v_held, sem_k, sem_v, sem_out):
    copies = []
    for slot, ref in enumerate((first_ref, second_ref)):
        rows = pl.ds(slot * ROWS, ROWS)
        copies.append((
            pltpu.make_async_copy(ref.at[2], v_held.at[slot], sem_v.at[slot]),
            pltpu.make_async_copy(ref.at[1], held.at[:, 0, rows, :], sem_k.at[slot]),
        ))
        copies[-1][0].start()
        copies[-1][1].start()
    for slot in range(2):
        copies[slot][0].wait()
        for head in range(GROUP):
            for block in range(0, ROWS, BLK):
                rows = pl.ds(slot * ROWS + block, BLK)
                held[head, 1, rows, :] = v_held[slot, head, block:block + BLK, :].T
    for slot in range(2):
        copies[slot][1].wait()
    copy = pltpu.make_async_copy(held, out_ref, sem_out)
    copy.start()
    copy.wait()


def place_group(order, where, slot, held, out_ref, sem):
    group = lax.rem(where[2] + slot, RING)
    for place in range(GROUP):
        pltpu.make_async_copy(
            held.at[place], out_ref.at[:, columns(order[group * GROUP + place])], sem
        ).start()


def place_rest(order, where, *refs):
    count = RING - 1
    parts, (_, out_ref, held, sem_in, sem_out, _) = refs[:count], refs[count:]
    copies = [
        pltpu.make_async_copy(parts[i], held.at[i], sem_in.at[i]) for i in range(count)
    ]
    for copy in copies:
        copy.start()
    for i, copy in enumerate(copies):
        copy.wait()
        place_group(order, where, i + 1, held.at[i], out_ref, sem_out)
    pltpu.make_async_copy(held, held, sem_out).wait()


def first_block(where, slot, offset):
    place = lax.rem(where[2] - slot + RING, RING)
    ring = lax.rem(where[1] + offset, RING)
    return jnp.where(where[0] == 0, ring * RING + place, place * RING + ring) * HALVES


def mark_queries(where, mask_ref, q_refs, kv_refs, marked_ref):
    lane = lax.broadcasted_iota(jnp.int32, (1, BLOCKS), 1)
    wide = lax.broadcasted_iota(jnp.int32, (BLK, HEAD), 1)
    for slot in range(RING):
        for half in range(HALVES):
            block = first_block(where, slot, 0) + half
            line = mask_ref[0, pl.ds(block, 1), :]
            line = jnp.where((line == 1) | (lane == block), 0.0, NEG)
            line = jnp.concatenate([line, jnp.zeros((1, HEAD - BLOCKS), F32)], axis=1)
            rows = pl.ds((slot - 1) % RING * ROWS + half * BLK, BLK)
            query = q_refs[slot][0, 0, half * BLK:(half + 1) * BLK, :]
            key = kv_refs[slot // 2][0, 0, pl.ds(slot % 2 * ROWS + half * BLK, BLK), :]
            level = jnp.sum(
                query.astype(F32) * key.astype(F32), axis=1, keepdims=True
            )
            mark = jnp.where(wide == LEVEL, -level, jnp.broadcast_to(line, (BLK, HEAD)))
            marked_ref[0, rows, :HEAD] = query
            marked_ref[0, rows, HEAD:] = mark.astype(BF16)


def mark_keys(where, offset, half, marks):
    lane = lax.broadcasted_iota(jnp.int32, (ROWS, HEAD), 1)
    line = lax.broadcasted_iota(jnp.int32, (ROWS, HEAD), 0) // BLK
    for i in range(2):
        block = first_block(where, 2 * half + i, offset) + line
        mark = jnp.where((lane == block) | (lane == LEVEL), 1.0, 0.0)
        marks[i * ROWS:(i + 1) * ROWS, :] = mark.astype(BF16)


def turned(kv_ref, *lead):
    return jnp.concatenate(
        [kv_ref[(*lead, 1, pl.ds(block, BLK))] for block in range(0, HALF, BLK)], axis=1
    )


def attend_again(head, where, marked_ref, chunks, kv_all, out_refs, marks, kv, sem):
    tokens = marked_ref.shape[1]
    lane = lax.broadcasted_iota(jnp.int32, (tokens, 2 * HEAD), 1)
    query = marked_ref[0]
    query = jnp.where(lane == HEAD + LEVEL, jnp.zeros_like(query), query)

    def step(turn, carry):
        top, sums, total = carry
        offset, half = jnp.int32(0), jnp.int32(0)
        for i, (one, other) in enumerate(chunks):
            offset = jnp.where(turn == i, one, offset)
            half = jnp.where(turn == i, other, half)

            @pl.when(turn == i)
            def _(i=i):
                copy = pltpu.make_async_copy(kv_all[i].at[head], kv, sem)
                copy.start()
                copy.wait()

        mark_keys(where, offset, half, marks)
        scores = lax.dot_general(
            jnp.concatenate([kv[0], marks[...]], axis=1),
            query,
            (((1,), (1,)), ((), ())),
            preferred_element_type=F32,
        )
        new = jnp.maximum(top, jnp.max(scores, axis=0, keepdims=True))
        weights = jnp.exp2((scores - new) * LOG2_SCALE).astype(BF16)
        decay = jnp.exp2((top - new) * LOG2_SCALE)
        sums = sums * decay + jnp.sum(weights.astype(F32), axis=0, keepdims=True)
        total = total * decay + jnp.dot(turned(kv), weights, preferred_element_type=F32)
        return new, sums, total

    start = (
        jnp.full((1, tokens), -3e38, F32),
        jnp.zeros((1, tokens), F32),
        jnp.zeros((HEAD, tokens), F32),
    )
    _, sums, total = lax.fori_loop(0, len(chunks), step, start)
    store(total / sums, out_refs)


def store(result, out_refs):
    for i, ref in enumerate(out_refs):
        ref[0] = result[:, i * ROWS:(i + 1) * ROWS].T.astype(BF16)


def attend(chunks, everything, tail, order, where, *refs):
    count = len(chunks)
    first, last = chunks[0][0] == 0, everything is not None
    kv_refs, refs = refs[:count], refs[count:]
    if first:
        mask_ref, q_refs, refs = refs[0], refs[1:1 + RING], refs[1 + RING:]
        marked_ref, state_ref, marks = refs
        mark_queries(where, mask_ref, q_refs, kv_refs, marked_ref)
        states = [jnp.zeros((HEAD + 8, TOKENS), F32)]
    else:
        marked_ref, before_ref, refs = refs[0], refs[1], refs[2:]
        if tail:
            kv_all, time_ref, refs = refs[:len(everything)], refs[len(everything)], refs[len(everything) + 1:]
            out_ref, marks, marks_more, kv, sem, own_held, time_held, sem_time, sem_own = refs
            time = pltpu.make_async_copy(time_ref, time_held, sem_time.at[0])
            time.start()
        elif last:
            kv_all, refs = refs[:len(everything)], refs[len(everything):]
            out_refs, (marks, marks_more, kv, sem) = refs[:RING - 1], refs[RING - 1:]
        else:
            state_ref, marks = refs

    @pl.when(pl.program_id(0) == 0)
    def _():
        for i, (offset, half) in enumerate(chunks):
            mark_keys(where, offset, half, marks.at[pl.ds(i * HALF, HALF)])

    heads = range(GROUP if tail else 1)
    if not first:
        states = [before_ref[head] for head in heads]
    ones = jnp.ones((8, TOKENS), BF16)
    for i in range(0, count, 2):
        pair = kv_refs[i:i + 2]
        scores = []
        for head in heads:
            keys = jnp.concatenate([kv_ref[head, 0] for kv_ref in pair], axis=0)
            scores.append(lax.dot_general(
                jnp.concatenate([keys, marks[i * HALF:(i + 2) * HALF]], axis=1),
                marked_ref[head],
                (((1,), (1,)), ((), ())),
                preferred_element_type=F32,
            ))
        weights = [jnp.exp2(score * LOG2_SCALE).astype(BF16) for score in scores]
        for head in heads:
            vals = jnp.concatenate([turned(kv_ref, head) for kv_ref in pair], axis=1)
            states[head] += jnp.dot(
                jnp.concatenate([vals, ones], axis=0),
                weights[head],
                preferred_element_type=F32,
            )
    if not last:
        state_ref[0] = states[0]
        return
    if tail:
        time.wait()
        for place in range(TEMP_HEADS):
            pltpu.make_async_copy(
                time_held.at[:, pl.ds(place * HEAD, HEAD)],
                out_ref.at[:, columns(order[SPAT_HEADS + place])],
                sem_time.at[1],
            ).start()
    for head in heads:
        if tail:
            out_refs = [own_held.at[pl.ds(head, 1)]]
        state = states[head]
        sums = state[HEAD:HEAD + 1]
        store(state[:HEAD] / sums, out_refs)
        fine = jnp.max(jnp.where(sums < LARGE, 0.0, 1.0)) == 0.0

        @pl.when(jnp.logical_not(fine))
        def _(head=head, out_refs=out_refs):
            attend_again(
                head if tail else pl.program_id(0), where, marked_ref.at[pl.ds(head, 1)],
                everything, kv_all, out_refs, marks_more, kv, sem,
            )

        if tail:
            spatial = order[where[2] * GROUP + head]
            pltpu.make_async_copy(
                own_held.at[head], out_ref.at[:, columns(spatial)], sem_own
            ).start()
    if tail:
        pltpu.make_async_copy(time_held, time_held, sem_time.at[1]).wait()
        pltpu.make_async_copy(own_held, own_held, sem_own).wait()


def attention(held, chunks, order, where, mask=None, queries=(), carried=(), everything=None, time=None):
    several = 1 if time is None else GROUP

    def at(_, *block):
        zeros = (0,) * len(block)
        return pl.BlockSpec((several,) + block, lambda h, o, w: (h,) + zeros)

    count = len(chunks)
    slot_spec = at(1, ROWS, HEAD)
    tokens, start = TOKENS, 0
    if everything is not None:
        tokens, start = (TOKENS - ROWS, 0) if time is None else (ROWS, RING - 1)
    marked_spec = pl.BlockSpec((several, tokens, 2 * HEAD), lambda h, o, w: (h, start, 0))
    state_spec = pl.BlockSpec((several, HEAD + 8, tokens), lambda h, o, w: (h, 0, start))
    in_specs = [at(1, 2, HALF, HEAD)] * count
    marked_shape = jax.ShapeDtypeStruct((GROUP, TOKENS, 2 * HEAD), BF16)
    state_shape = jax.ShapeDtypeStruct((GROUP, HEAD + 8, TOKENS), F32)
    scratch = [pltpu.VMEM((count * HALF, HEAD), BF16)]
    extra = []
    if queries:
        extra = [mask]
        in_specs += [
            pl.BlockSpec((1, BLOCKS, BLOCKS), lambda h, o, w: (o[w[2] * GROUP + h], 0, 0))
        ]
        in_specs += [
            pl.BlockSpec((1, 1, ROWS, HEAD), lambda h, o, w: (0, h, 0, 0))
        ] * RING
        out_specs, out_shape = [marked_spec, state_spec], [marked_shape, state_shape]
    else:
        in_specs += [marked_spec, state_spec]
        out_specs, out_shape = state_spec, state_shape
    every = []
    if everything is not None:
        every = [held[chunk] for chunk in everything]
        in_specs += [HBM] * len(every)
        scratch += [pltpu.VMEM((HALF, HEAD), BF16), pltpu.VMEM((2, HALF, HEAD), BF16), DMA]
        if time is None:
            out_specs = [slot_spec] * (RING - 1)
            out_shape = [jax.ShapeDtypeStruct((GROUP, ROWS, HEAD), BF16)] * (RING - 1)
        else:
            every.append(time)
            in_specs += [HBM]
            out_specs = HBM
            out_shape = jax.ShapeDtypeStruct((ROWS, HEADS * HEAD), BF16)
            scratch += [pltpu.VMEM((GROUP, ROWS, HEAD), BF16)]
            scratch += [pltpu.VMEM((ROWS, TEMP_HEADS * HEAD), BF16), DMAS, DMA]
    hint = H0 if queries else H1 if everything is None else 2 if time is None else 1
    flops = hint * 8 * GROUP * tokens * count * HALF * HEAD
    return pl.pallas_call(
        functools.partial(attend, chunks, everything, time is not None),
        grid_spec=pltpu.PrefetchScalarGridSpec(
            num_scalar_prefetch=2,
            grid=(GROUP // several,),
            in_specs=in_specs,
            out_specs=out_specs,
            scratch_shapes=scratch,
        ),
        out_shape=out_shape,
        compiler_params=PARAMS,
        cost_estimate=pl.CostEstimate(flops=flops, bytes_accessed=4 << 20, transcendentals=0),
        name="spatial_attention",
    )(order, where, *[held[chunk] for chunk in chunks], *extra, *queries, *carried, *every)


def attend_time(order, mask_ref, valid_ref, q_ref, k_ref, v_ref, out_ref):
    lane = lax.broadcasted_iota(jnp.int32, (ROWS, HEAD), 1)
    row = lax.broadcasted_iota(jnp.int32, (ROWS, HEAD), 0)
    frame, place = row // PART, row % PART
    here = lane == FRAMES + place
    inside = (lane >= FRAMES) & (lane < FRAMES + PART)
    key_mark = jnp.where(lane == frame, 1.0, jnp.where(inside & ~here, NEG, 0.0)).astype(BF16)
    ones = jnp.ones((ROWS, HEAD), BF16)
    short = lax.broadcasted_iota(jnp.int32, (FRAMES, FRAMES), 1)
    same = short == lax.broadcasted_iota(jnp.int32, (FRAMES, FRAMES), 0)
    which = lax.broadcasted_iota(jnp.int32, mask_ref.shape, 2)
    every = range(TIME_STEP)
    at = [slice(slot * HEAD, (slot + 1) * HEAD) for slot in every]
    scores = []
    for slot in every:
        head = order[SPAT_HEADS + pl.program_id(0) * TIME_STEP + slot]
        seen = jnp.sum(jnp.where(which == head, mask_ref[...], 0), axis=2)
        seen = (seen == 1) & (valid_ref[...] == 1)
        pairs = jnp.where(seen | same, 0.0, NEG)
        pairs = jnp.concatenate([pairs, jnp.zeros((FRAMES, HEAD - FRAMES), F32)], axis=1)
        pairs = jnp.broadcast_to(pairs[:, None, :], (FRAMES, PART, HEAD)).reshape(ROWS, HEAD)
        mark = jnp.where(here, 1.0, pairs).astype(BF16)
        query = jnp.concatenate([q_ref[:, at[slot]], mark], axis=1)
        keys = jnp.concatenate([k_ref[:, at[slot]], key_mark], axis=1)
        scores.append(
            lax.dot_general(query, keys, (((1,), (1,)), ((), ())), preferred_element_type=F32)
        )
    tops = [jnp.max(scores[slot], axis=1, keepdims=True) for slot in every]
    weights = [
        jnp.exp2((scores[slot] - tops[slot]) * LOG2_SCALE).astype(BF16) for slot in every
    ]
    for slot in every:
        vals = jnp.concatenate([v_ref[:, at[slot]], ones], axis=1)
        both = jnp.dot(weights[slot], vals, preferred_element_type=F32)
        out_ref[:, at[slot]] = (both[:, :HEAD] / both[:, HEAD:]).astype(BF16)


def time_attention(order, mask, valid, gathered):
    steps = TEMP_HEADS // TIME_STEP

    def at(which):
        return pl.BlockSpec((ROWS, TIME_STEP * HEAD), lambda h, o: (0, which * steps + h))

    return pl.pallas_call(
        attend_time,
        grid_spec=pltpu.PrefetchScalarGridSpec(
            num_scalar_prefetch=1,
            grid=(steps,),
            in_specs=[
                pl.BlockSpec(mask.shape, lambda h, o: (0, 0, 0)),
                pl.BlockSpec(valid.shape, lambda h, o: (0, 0)),
            ]
            + [at(which) for which in range(3)],
            out_specs=at(0),
        ),
        out_shape=jax.ShapeDtypeStruct((ROWS, TEMP_HEADS * HEAD), BF16),
        compiler_params=PARAMS,
        cost_estimate=pl.CostEstimate(flops=3 << 30, bytes_accessed=4 << 20, transcendentals=0),
        name="temporal_attention",
    )(order, mask, valid, gathered, gathered, gathered)


def call(body, name, moved, in_specs, out_specs, out_shape, scratch, *args, **more):
    return pl.pallas_call(
        body,
        in_specs=in_specs,
        out_specs=out_specs,
        out_shape=out_shape,
        scratch_shapes=scratch,
        compiler_params=PARAMS,
        cost_estimate=pl.CostEstimate(flops=0, bytes_accessed=moved << 20, transcendentals=0),
        name=name,
        **more,
    )(*args)


def shards(queries, keys, values, head_kind, spatial_mask, temporal_mask, frame_valid):
    rows, width = queries.shape[1:]
    queries, keys, values = (t.reshape(rows, width) for t in (queries, keys, values))
    slot_shape = (GROUP, ROWS, HEAD)
    three_shape = (3,) + slot_shape
    wide_shape = (ROWS, 3 * TEMP_HEADS * HEAD)
    *threes, order, where = call(
        pack_spatial,
        "pack_spatial",
        5,
        [SMEM, HBM, HBM, HBM],
        [HBM] * (RING - 1) + [SMEM] * 2,
        [jax.ShapeDtypeStruct(three_shape, BF16)] * (RING - 1)
        + [jax.ShapeDtypeStruct((HEADS,), jnp.int32), jax.ShapeDtypeStruct((3,), jnp.int32)],
        [pltpu.VMEM((RING - 1,) + three_shape, BF16), DMAS, DMAS],
        head_kind, queries, keys, values,
    )
    threes = [shift(threes[s - 1], s, True) for s in range(1, RING)]
    own_three, packed = call(
        pack_rest,
        "pack_rest",
        40,
        [SMEM] * 2 + [HBM] * 3,
        [HBM] * 2,
        [jax.ShapeDtypeStruct(three_shape, BF16), jax.ShapeDtypeStruct(wide_shape, BF16)],
        [pltpu.VMEM(three_shape, BF16), pltpu.VMEM(wide_shape, BF16)] + [DMAS] * 3,
        order, where, queries, keys, values,
    )
    threes = [own_three] + threes
    gathered = lax.all_to_all(packed, "frame", 0, 0, tiled=True)

    half_shape = (GROUP, 2, HALF, HEAD)
    held = {}
    for half in range(2):
        held[0, half] = call(
            join,
            "join",
            2,
            [HBM] * 2,
            HBM,
            jax.ShapeDtypeStruct(half_shape, BF16),
            [pltpu.VMEM(half_shape, BF16), pltpu.VMEM((2,) + slot_shape, BF16), DMAS, DMAS, DMA],
            *threes[2 * half:2 * half + 2],
        )
        if half == 0:
            held[0, 0], threes[2], threes[3] = lax.optimization_barrier(
                (held[0, 0], threes[2], threes[3])
            )
    left, right, far = RING - 1, 1, 2
    held[left, 0] = shift(held[0, 0], 1, False)
    held[right, 1] = shift(held[0, 1], RING - 1, False)
    held[left, 1] = shift(held[0, 1], 1, False)
    held[right, 0] = shift(held[0, 0], RING - 1, False)
    marked, state = attention(
        held, [(0, 0), (0, 1)], order, where, mask=spatial_mask, queries=threes
    )
    held[far, 0] = shift(held[left, 0], 1, False)
    held[far, 1] = shift(held[right, 1], RING - 1, False)
    state = attention(held, [(left, 0), (right, 1)], order, where, carried=(marked, state))
    time_out = time_attention(
        order, jnp.transpose(temporal_mask, (1, 2, 0)), frame_valid[None], gathered
    )
    time_out = lax.all_to_all(time_out, "frame", 0, 0, tiled=True)
    chunks = [(left, 1), (right, 0), (far, 0), (far, 1)]
    everything = [(offset, half) for offset in (0, left, right, far) for half in range(2)]
    finish = functools.partial(
        attention, held, chunks, order, where, carried=(marked, state), everything=everything
    )
    parts = finish()
    parts = [shift(parts[s - 1], RING - s, True) for s in range(1, RING)]
    base = finish(time=time_out)
    result = call(
        place_rest,
        "place_rest",
        1,
        [SMEM, SMEM] + [HBM] * RING,
        HBM,
        jax.ShapeDtypeStruct((rows, width), BF16),
        [
            pltpu.VMEM((RING - 1,) + slot_shape, BF16),
            DMAS,
            DMA,
            pltpu.VMEM((FILLER, HEAD), F32),
        ],
        order, where, *parts, base,
        input_output_aliases={1 + RING: 0},
    )
    return result[None]


def solution(mesh):
    wide = P("frame", "region", None)
    return jax.shard_map(
        shards,
        mesh=mesh,
        in_specs=(wide, wide, wide, P(), P(), P(), P()),
        out_specs=wide,
        check_vma=False,
    )
```
